512 devices in a mesh: dp: 128 (over z, y, core), group: 4 (over x).
Axes of the slice: x: 4, y: 8, z: 8, core: 2. Of those that a mesh axis runs over, the one named last changes fastest.
Arguments:
- tokens: bfloat16 [81920, 1280], P('dp', 'group'), may hold values from -40 to 40
- cotangent: bfloat16 [81920, 1280], P('dp', 'group'), may hold values from -6 to 6
- slot_table: int32 [640, 2], replicated, may hold values from -1 to 128, as said below
- w_qkv: bfloat16 [1280, 1920], P(None, 'group'), may hold values from -0.15625 to 0.15625
- qkv_bias: float32 [1920], P('group'), may hold values from -3 to 3
- w_out: bfloat16 [640, 1280], P('group'), may hold values from -0.625 to 0.625
- out_bias: float32 [1280], P('group'), may hold values from -3 to 3
Outputs:
- layer_out: bfloat16 [81920, 1280], P('dp', 'group')
- input_grad: bfloat16 [81920, 1280], P('dp', 'group')
- w_qkv_grad: bfloat16 [1280, 1920], P(None, 'group')
- qkv_bias_grad: float32 [1920], P('group')
- w_out_grad: bfloat16 [640, 1280], P('group')
- out_bias_grad: float32 [1280], P('group')
The draws below stay inside these ranges and needn't reach their ends.
Inputs may be any that keep to these rules, and one draw needn't show every extreme that they name: `slot_table`: column 0 is the patch count of each home image slot of each dp index: 0 for an empty slot, else 128/4 to 128. Column 1 says where the image is processed: p below 3 means on its own dp index in processing slot p; 3 + p, with p below 2, means on the dp index half the axis away, in that index's processing slot p; -1 for an empty slot. Every dp index holds 1 to 5 images and every processing slot of every dp index receives exactly one image. Only an index holding more than 3 images sends images away, at most 2 of them, and its partner then holds fewer than 3.
All inputs are finite; a program needn't handle non-finite values.
Results may differ from the reference program's by a relative error of at most 0.027.
The reference program's roundings to bfloat16 on the way count: a program that leaves them out, or rounds other values in their place, can miss the bound.
Values may be sent and summed in bfloat16 or wider, within the bound.
A program may use at most 64 MiB of HBM per device.

```python
import math
import jax
import jax.numpy as jnp
from jax import lax

D = 1280
HEADS = 8
HD = 80
IMG = 128
PROC = 3
HOME = 5
TOKENS = 81920
N_DP = 128
N_GROUP = 4


def draw_tokens(key, part):
    key = jax.random.fold_in(key, 11)
    key_list = jax.random.split(key, 1)
    images = N_DP * HOME
    base = jnp.clip(jax.random.normal(key_list[0], (images, IMG, D), jnp.float32), -4.0, 4.0)
    return base.reshape(images * IMG, D).astype(jnp.bfloat16)


def permute_rows(key, count, length):
    subkeys = jax.random.split(key, count)
    return jax.vmap(jax.random.permutation, in_axes=(0, None))(subkeys, length)


def draw_slot_table(key, part):
    key = jax.random.fold_in(key, 23)
    key_list = jax.random.split(key, 8)
    pairs = N_DP // 2
    pair_index = jnp.arange(pairs)
    heavy_side = jax.random.randint(key_list[0], (pairs,), 0, 2)
    moved_count = jax.random.randint(key_list[1], (pairs,), 1, PROC)
    moved_count = jnp.where(pair_index == 0, PROC - 1, moved_count)[:, None]
    keep_order = permute_rows(key_list[2], pairs, PROC)
    land_front = permute_rows(key_list[3], pairs, PROC - 1)
    reverse_slots = PROC - 2 - jnp.arange(PROC - 1)
    land_front = jnp.where(pair_index[:, None] == 0, reverse_slots[None, :], land_front)
    last_slot = jnp.full((pairs, 1), PROC - 1, land_front.dtype)
    land_order = jnp.concatenate([land_front, last_slot], axis=1)
    heavy_rank = jnp.argsort(permute_rows(key_list[4], pairs, HOME), axis=1)
    light_rank = jnp.argsort(permute_rows(key_list[5], pairs, HOME), axis=1)
    kept_at = jnp.take_along_axis(keep_order, jnp.clip(heavy_rank, 0, PROC - 1), axis=1)
    sent_at = jnp.take_along_axis(land_order, jnp.clip(heavy_rank - PROC, 0, PROC - 1), axis=1)
    heavy_place = jnp.where(heavy_rank < PROC, kept_at, jnp.where(heavy_rank < PROC + moved_count, PROC + sent_at, -1))
    light_at = jnp.take_along_axis(land_order, jnp.clip(moved_count + light_rank, 0, PROC - 1), axis=1)
    light_place = jnp.where(light_rank < PROC - moved_count, light_at, -1)
    heavy_size = jax.random.randint(key_list[6], (pairs, HOME), IMG // 4, IMG + 1)
    light_size = jax.random.randint(key_list[7], (pairs, HOME), IMG // 4, IMG + 1)
    heavy_count = jnp.where(heavy_place >= 0, jnp.where(heavy_rank == 0, IMG, heavy_size), 0)
    light_count = jnp.where(light_place >= 0, jnp.where(light_rank == 0, IMG, light_size), 0)
    lower_heavy = heavy_side[:, None] == 0
    lower_place = jnp.where(lower_heavy, heavy_place, light_place)
    upper_place = jnp.where(lower_heavy, light_place, heavy_place)
    lower_count = jnp.where(lower_heavy, heavy_count, light_count)
    upper_count = jnp.where(lower_heavy, light_count, heavy_count)
    place_all = jnp.concatenate([lower_place, upper_place], axis=0).reshape(-1)
    count_all = jnp.concatenate([lower_count, upper_count], axis=0).reshape(-1)
    return jnp.stack([count_all, place_all], axis=1).astype(jnp.int32)


def steps_of(key, extent, pieces, least, high):
    def one(axis_at, shards_of):
        draws = jax.random.uniform(jax.random.fold_in(jax.random.fold_in(key, 6), axis_at), (shards_of,), jnp.float32, least / len(pieces), high / len(pieces))
        return jnp.repeat(jnp.exp(draws), extent[axis_at] // shards_of).reshape((-1,) + (1,) * (len(extent) - axis_at - 1))

    gain = one(*pieces[0])
    for cut in pieces[1:]:
        gain = gain * one(*cut)
    return gain


def centred(own_key, dims, spread, bound, cuts=(), held_as=jnp.bfloat16):
    factor_of = steps_of(own_key, dims, cuts, -0.22, 0.18) if cuts else 1.0
    values = jax.random.normal(own_key, dims, jnp.float32) * spread * factor_of
    return jnp.minimum(jnp.maximum(values, -bound), bound).astype(held_as)


def setup_inputs(seed: int = 0) -> dict:
    streams_of = jax.random.split(jax.random.key(seed), 8)
    tokens = draw_tokens(jax.random.fold_in(streams_of[7], 71), 0)
    cotangent = centred(streams_of[1], (TOKENS, D), 1.0, 6.0, ((0, 128), (1, 4)))
    slot_table = draw_slot_table(jax.random.fold_in(streams_of[7], 71), 0)
    w_qkv = centred(streams_of[3], (D, 3 * HEADS * HD), D ** -0.5, 0.15625, ((1, 4),))
    qkv_bias = centred(streams_of[4], (3 * HEADS * HD,), 0.5, 3.0, ((0, 4),), jnp.float32)
    w_out = centred(streams_of[5], (HEADS * HD, D), HD ** -0.5, 0.625, ((0, 4),))
    out_bias = centred(streams_of[6], (D,), 0.5, 3.0, ((0, 4),), jnp.float32)
    return dict(tokens=tokens, cotangent=cotangent, slot_table=slot_table, w_qkv=w_qkv, qkv_bias=qkv_bias, w_out=w_out, out_bias=out_bias)


def rounded(value):
    return lax.optimization_barrier(value.astype(jnp.bfloat16)).astype(jnp.float32)

def image_pass(image_x, image_g, counts, w_qkv, qkv_bias, w_out, out_bias):
    slot_count = image_x.shape[0]
    row_count = slot_count * IMG
    per_group = HEADS // N_GROUP
    highest = lax.Precision.HIGHEST
    row_valid = jnp.arange(IMG).astype(jnp.int32)[None, :] < counts[:, None]
    mask_rows = row_valid.reshape(row_count, 1)
    flat_x = image_x.reshape(row_count, D)
    flat_g = jnp.where(mask_rows, image_g.reshape(row_count, D), jnp.zeros((), jnp.bfloat16))
    projected = rounded(jnp.dot(flat_x, w_qkv, preferred_element_type=jnp.float32) + qkv_bias)
    projected = projected.reshape(slot_count, IMG, HEADS, 3, HD)
    queries = projected[:, :, :, 0]
    key_rows = projected[:, :, :, 1]
    values = projected[:, :, :, 2]
    score_scale = 1.0 / math.sqrt(HD)
    scores = jnp.einsum('sihe,sjhe->shij', queries, key_rows, precision=highest) * score_scale
    scores = jnp.where(row_valid[:, None, None, :], scores, -1e+30)
    row_top = lax.optimization_barrier(jnp.max(scores, axis=-1, keepdims=True))
    exponent = jnp.exp(scores - row_top)
    attn_probs = exponent / lax.optimization_barrier(jnp.sum(exponent, axis=-1, keepdims=True))
    probs_b = rounded(attn_probs)
    mixed_b = jnp.einsum('shij,sjhe->sihe', probs_b, values, precision=highest).astype(jnp.bfloat16)
    mixed_b = lax.optimization_barrier(mixed_b.reshape(row_count, HEADS * HD))
    mixed = mixed_b.astype(jnp.float32)
    out_parts = jnp.einsum('rgc,gcd->grd', mixed.reshape(row_count, N_GROUP, per_group * HD), w_out.astype(jnp.float32).reshape(N_GROUP, per_group * HD, D), precision=highest)
    branch = lax.optimization_barrier(jnp.sum(rounded(out_parts), axis=0))
    layer_out = jnp.where(mask_rows, flat_x.astype(jnp.float32) + branch + out_bias, 0.0).astype(jnp.bfloat16)
    grad_float = flat_g.astype(jnp.float32)
    out_bias_grad = lax.optimization_barrier(jnp.sum(grad_float, axis=0))
    w_out_grad = jnp.dot(mixed_b.T, flat_g, preferred_element_type=jnp.float32)
    grad_mixed = rounded(jnp.dot(flat_g, w_out.T, preferred_element_type=jnp.float32))
    grad_mixed = grad_mixed.reshape(slot_count, IMG, HEADS, HD)
    grad_probs = jnp.einsum('sihe,sjhe->shij', grad_mixed, values, precision=highest)
    inner = lax.optimization_barrier(jnp.sum(attn_probs * grad_probs, axis=-1, keepdims=True))
    grad_scores = rounded(attn_probs * (grad_probs - inner) * score_scale)
    grad_query = jnp.einsum('shij,sjhe->sihe', grad_scores, key_rows, precision=highest)
    grad_keys = jnp.einsum('shij,sihe->sjhe', grad_scores, queries, precision=highest)
    grad_values = jnp.einsum('shij,sihe->sjhe', probs_b, grad_mixed, precision=highest)
    grad_proj = jnp.stack([grad_query, grad_keys, grad_values], axis=3).reshape(row_count, 3 * HEADS * HD)
    qkv_bias_grad = lax.optimization_barrier(jnp.sum(grad_proj, axis=0))
    grad_proj_b = lax.optimization_barrier(grad_proj.astype(jnp.bfloat16))
    w_qkv_grad = jnp.dot(flat_x.T, grad_proj_b, preferred_element_type=jnp.float32)
    input_parts = jnp.einsum('rgc,dgc->grd', grad_proj_b.astype(jnp.float32).reshape(row_count, N_GROUP, per_group * 3 * HD), w_qkv.astype(jnp.float32).reshape(D, N_GROUP, per_group * 3 * HD), precision=highest)
    input_sum = lax.optimization_barrier(jnp.sum(rounded(input_parts), axis=0))
    input_grad = jnp.where(mask_rows, grad_float + input_sum, 0.0).astype(jnp.bfloat16)
    return (layer_out, input_grad, (w_qkv_grad, qkv_bias_grad, w_out_grad, out_bias_grad))

def reference(tokens, cotangent, slot_table, w_qkv, qkv_bias, w_out, out_bias):
    counts = slot_table[:, 0].astype(jnp.int32).reshape(N_DP, HOME)
    token_blocks = tokens.reshape(N_DP, HOME, IMG, D)
    grad_blocks = cotangent.reshape(N_DP, HOME, IMG, D)

    def step(totals, block_item):
        block_x, block_g, block_counts = block_item
        layer_out, input_grad, grads = image_pass(block_x, block_g, block_counts, w_qkv, qkv_bias, w_out, out_bias)
        return (jax.tree.map(jnp.add, totals, grads), (layer_out, input_grad))
    initial = (jnp.zeros((D, 3 * HEADS * HD), jnp.float32), jnp.zeros((3 * HEADS * HD,), jnp.float32), jnp.zeros((HEADS * HD, D), jnp.float32), jnp.zeros((D,), jnp.float32))
    totals, outputs = lax.scan(step, initial, (token_blocks, grad_blocks, counts))
    grad_scale = 1.0 / math.sqrt(N_DP * HOME * IMG)
    return (outputs[0].reshape(TOKENS, D), outputs[1].reshape(TOKENS, D), (totals[0] * grad_scale).astype(jnp.bfloat16), totals[1] * grad_scale, (totals[2] * grad_scale).astype(jnp.bfloat16), totals[3] * grad_scale)
```

```python
import functools
import math

import jax
import jax.numpy as jnp
from jax import lax
from jax.experimental import pallas as pl
from jax.experimental.pallas import tpu as pltpu
from jax.sharding import PartitionSpec as P

HD = 80
IMG = 128
MESH = pl.DeviceIdType.MESH
BF16 = jnp.bfloat16
F32 = jnp.float32


def far_first(n):
    return sorted(range(1, n), key=lambda k: (-min(k, n - k), k))


def comm_kernel(
    n, nb, nb2, slots, scale,
    cnt_ref, op_ref, ip_ref, g_ref, x_ref, gi_ref, bias_ref,
    lo_ref, ig_ref, f_ref,
    r0, s1, r1, t, r2, v, fw, mrg, rcv,
    b0s, b0r, b1s, b1r, b2s, b2r, b3s, b3r, b4s, b4r, b5s, b5r,
    xs, xr,
):
    dp = lax.axis_index("dp")
    grp = lax.axis_index("group")
    c = lax.rem(dp, 2)
    y = lax.rem(lax.div(dp, 2), n)
    z = lax.div(dp, 2 * n)
    other = dp + 1 - 2 * c
    gr = lax.rem(grp + 1, 4)
    gl = lax.rem(grp + 3, 4)
    me = (y, z)

    def on_axis(axis, idx):
        return (z * n + idx) * 2 + c if axis == 0 else (idx * n + y) * 2 + c

    def plus(a, k):
        return lax.rem(a + k, n)

    def send(src, dst, ss, rs, d, g):
        return pltpu.make_async_remote_copy(
            src_ref=src, dst_ref=dst, send_sem=ss, recv_sem=rs,
            device_id=(d, g), device_id_type=MESH,
        )

    barrier = pltpu.get_barrier_semaphore()
    pl.semaphore_signal(barrier, inc=1, device_id=(other, grp), device_id_type=MESH)
    for axis in (0, 1):
        for k in range(1, n):
            pl.semaphore_signal(
                barrier, inc=1, device_id=(on_axis(axis, plus(me[axis], k)), grp),
                device_id_type=MESH,
            )
    for g in (gr, gl):
        pl.semaphore_signal(barrier, inc=1, device_id=(dp, g), device_id_type=MESH)
    pl.semaphore_wait(barrier, 1 + 2 * (n - 1) + 2)

    order = far_first(n) + [0]

    def l0(s, k):
        p = plus(me[s], k)
        return send(g_ref.at[1 - c, s, p], r0.at[s, p], b0s.at[s, k], b0r.at[s, k], other, grp)

    for k in order:
        for s in (0, 1):
            l0(s, k).start()

    half = IMG // 2
    gx = lax.rem(grp + 2, 4)

    def x_copy(arr, img, j):
        src = (op_ref, ip_ref)[arr]
        ch = arr * slots + img
        lo = pl.ds(img * IMG, half)
        hi = pl.ds(img * IMG + half, half)
        return (
            lambda: send(src.at[gx, lo], fw.at[ch, 0], xs.at[ch, 0], xr.at[ch, 0], dp, gr),
            lambda: send(src.at[gx, hi], fw.at[ch, 1], xs.at[ch, 1], xr.at[ch, 1], dp, gl),
            lambda: send(src.at[gr, hi], rcv.at[ch, 0, 1], xs.at[ch, 2], xr.at[ch, 2], dp, gr),
            lambda: send(src.at[gl, lo], rcv.at[ch, 1, 0], xs.at[ch, 3], xr.at[ch, 3], dp, gl),
            lambda: send(mrg.at[ch, 0], rcv.at[ch, 0, 0], xs.at[ch, 4], xr.at[ch, 4], dp, gr),
            lambda: send(mrg.at[ch, 1], rcv.at[ch, 1, 1], xs.at[ch, 5], xr.at[ch, 5], dp, gl),
        )[j]()

    for arr in (0, 1):
        def raw(img, _, arr=arr):
            for j in range(4):
                x_copy(arr, img, j).start()
            return 0
        lax.fori_loop(0, slots, raw, 0)

    def l1(s, k):
        return send(
            s1.at[s, k], r1.at[s, k], b1s.at[s, k], b1r.at[s, k],
            on_axis(s, plus(me[s], k)), grp,
        )

    for k in order:
        for s in (0, 1):
            l0(s, k).wait_recv()
            p = plus(me[s], k)
            total = g_ref[c, s, p] + r0[s, p]
            if k:
                s1[s, k] = total.astype(BF16)
                l1(s, k).start()
            else:
                t[s, pl.ds(0, nb)] = total
                if nb2 * n > nb:
                    t[s, pl.ds(nb, nb2 * n - nb)] = jnp.zeros((nb2 * n - nb, 16, 128), F32)

    def merge(arr):
        def step(img, _):
            ch = arr * slots + img
            src = (op_ref, ip_ref)[arr]
            x_copy(arr, img, 0).wait_recv()
            mine = src[gr, pl.ds(img * IMG, half)].astype(F32)
            mrg[ch, 0] = (mine + fw[ch, 0].astype(F32)).astype(BF16)
            x_copy(arr, img, 4).start()
            x_copy(arr, img, 1).wait_recv()
            mine = src[gl, pl.ds(img * IMG + half, half)].astype(F32)
            mrg[ch, 1] = (mine + fw[ch, 1].astype(F32)).astype(BF16)
            x_copy(arr, img, 5).start()
            return 0
        lax.fori_loop(0, slots, step, 0)

    merge(0)

    def l2(s, k):
        q = plus(me[1 - s], k)
        return send(
            t.at[s, pl.ds(q * nb2, nb2)], r2.at[s, k], b2s.at[s, k], b2r.at[s, k],
            on_axis(1 - s, q), grp,
        )

    near = list(reversed(far_first(n)))
    for s in (0, 1):
        for k in near:
            l1(s, k).wait_recv()
        total = t[s, pl.ds(0, nb)]
        for k in near:
            total = total + r1[s, k].astype(F32)
        t[s, pl.ds(0, nb)] = total
        for k in far_first(n):
            l2(s, k).start()

    merge(1)

    def l3(s, k):
        mine = v.at[s, pl.ds(me[1 - s] * nb2, nb2)]
        return send(
            mine, mine, b3s.at[s, k], b3r.at[s, k], on_axis(1 - s, plus(me[1 - s], k)), grp,
        )

    for s in (0, 1):
        for k in near:
            l2(s, k).wait_recv()
        total = t[s, pl.ds(me[1 - s] * nb2, nb2)]
        for k in near:
            total = total + r2[s, k]
        v[s, pl.ds(me[1 - s] * nb2, nb2)] = (total * scale).astype(BF16)
        for k in far_first(n):
            l3(s, k).start()

    def l4(s, k):
        return send(
            v.at[s, pl.ds(0, nb)], f_ref.at[c, s, me[s]], b4s.at[s, k], b4r.at[s, k],
            on_axis(s, plus(me[s], k)), grp,
        )

    def l5(s, k):
        piece = f_ref.at[c, s, plus(me[s], k)]
        return send(piece, piece, b5s.at[s, k], b5r.at[s, k], other, grp)

    def l3_in(s, k):
        src = v.at[s, pl.ds(plus(me[1 - s], n - k) * nb2, nb2)]
        return send(src, src, b3s.at[s, k], b3r.at[s, k], other, grp)

    for s in (0, 1):
        for k in near:
            l3_in(s, k).wait_recv()
        for k in far_first(n):
            l4(s, k).start()
        f_ref[c, s, me[s]] = v[s, pl.ds(0, nb)]
        l5(s, 0).start()

    def l4_in(s, k):
        dst = f_ref.at[c, s, plus(me[s], n - k)]
        return send(dst, dst, b4s.at[s, k], b4r.at[s, k], other, grp)

    for k in near:
        for s in (0, 1):
            l4_in(s, k).wait_recv()
            l5(s, n - k).start()

    def finish(arr):
        def step(img, _):
            ch = arr * slots + img
            for j in range(2, 6):
                x_copy(arr, img, j).wait_recv()
            rows_at = pl.ds(img * IMG, IMG)
            src = (op_ref, ip_ref)[arr]
            total = src[grp, rows_at].astype(F32)
            total = total + rcv[ch, 0].reshape(IMG, -1).astype(F32)
            total = total + rcv[ch, 1].reshape(IMG, -1).astype(F32)
            if arr == 0:
                total = total + x_ref[rows_at].astype(F32) + bias_ref[...]
            else:
                total = total + gi_ref[rows_at].astype(F32)
            row = lax.broadcasted_iota(jnp.int32, total.shape, 0)
            total = jnp.where(row < cnt_ref[img], total, 0.0).astype(BF16)
            (lo_ref, ig_ref)[arr][rows_at] = total
            return 0
        lax.fori_loop(0, slots, step, 0)

    finish(0)
    finish(1)

    def l5_in(s, k):
        piece = f_ref.at[1 - c, s, plus(me[s], k)]
        return send(piece, piece, b5s.at[s, k], b5r.at[s, k], other, grp)

    for k in range(n):
        for s in (0, 1):
            l5_in(s, k).wait_recv()
            l0(s, k).wait_send()
            l5(s, k).wait_send()
            if k:
                l1(s, k).wait_send()
                l2(s, k).wait_send()
                l3(s, k).wait_send()
                l4(s, k).wait_send()
    for arr in (0, 1):
        def done(img, _, arr=arr):
            for j in range(6):
                x_copy(arr, img, j).wait_send()
            return 0
        lax.fori_loop(0, slots, done, 0)


def reduce_all(n, slots, scale, cnt, out_parts, in_parts, grads, x, gi, bias):
    nb = grads.shape[3]
    nb2 = -(-nb // n)
    rows, width = x.shape
    vm = pl.BlockSpec(memory_space=pltpu.VMEM)
    dma = pltpu.SemaphoreType.DMA
    chunks = 2 * slots
    return pl.pallas_call(
        functools.partial(comm_kernel, n, nb, nb2, slots, scale),
        out_shape=(
            jax.ShapeDtypeStruct((rows, width), BF16),
            jax.ShapeDtypeStruct((rows, width), BF16),
            jax.ShapeDtypeStruct((2, 2, n, nb, 16, 128), BF16),
        ),
        in_specs=[pl.BlockSpec(memory_space=pltpu.SMEM)] + [vm] * 6,
        out_specs=(vm, vm, vm),
        scratch_shapes=[
            pltpu.VMEM((2, n, nb, 16, 128), F32),
            pltpu.VMEM((2, n, nb, 16, 128), BF16),
            pltpu.VMEM((2, n, nb, 16, 128), BF16),
            pltpu.VMEM((2, n * nb2, 16, 128), F32),
            pltpu.VMEM((2, n, nb2, 16, 128), F32),
            pltpu.VMEM((2, n * nb2, 16, 128), BF16),
            pltpu.VMEM((chunks, 2, IMG // 2, width), BF16),
            pltpu.VMEM((chunks, 2, IMG // 2, width), BF16),
            pltpu.VMEM((chunks, 2, 2, IMG // 2, width), BF16),
        ] + [dma((2, n))] * 12 + [dma((chunks, 6))] * 2,
        compiler_params=pltpu.CompilerParams(
            collective_id=0, has_side_effects=True, vmem_limit_bytes=50 * 2**20,
        ),
        cost_estimate=pl.CostEstimate(flops=10**6, bytes_accessed=10**7, transcendentals=0),
    )(cnt, out_parts, in_parts, grads, x, gi, bias)


def to_blocks(n, w_qkv_grad, w_out_grad, qkv_bias_grad, out_bias_grad):
    rows, cols = w_qkv_grad.shape
    wide = -(-cols // 128) * 128
    a = jnp.pad(w_qkv_grad, ((0, 0), (0, wide - cols)))
    a = a.reshape(rows // 16, 16, wide // 128, 128).transpose(0, 2, 1, 3).reshape(-1, 16, 128)
    r2, c2 = w_out_grad.shape
    b = w_out_grad.reshape(r2 // 16, 16, c2 // 128, 128).transpose(0, 2, 1, 3).reshape(-1, 16, 128)
    bias = jnp.concatenate([qkv_bias_grad, out_bias_grad])
    bias = jnp.pad(bias, (0, 2048 - bias.shape[0])).reshape(1, 16, 128)
    used = a.shape[0] + b.shape[0] + 1
    nb = -(-used // (4 * n))
    full = jnp.concatenate([a, b, bias, jnp.zeros((4 * n * nb - used, 16, 128), F32)])
    return full.reshape(2, 2, n, nb, 16, 128)


def from_blocks(full, rows, cols, r2, c2, nq, no):
    full = full.reshape(-1, 16, 128)
    wide = -(-cols // 128) * 128
    na = rows * wide // 2048
    n_b = r2 * c2 // 2048
    a = full[:na].reshape(rows // 16, wide // 128, 16, 128).transpose(0, 2, 1, 3)
    a = a.reshape(rows, wide)[:, :cols]
    b = full[na:na + n_b].reshape(r2 // 16, c2 // 128, 16, 128).transpose(0, 2, 1, 3).reshape(r2, c2)
    bias = full[na + n_b].reshape(-1).astype(F32)
    return a, b, bias[:nq], bias[nq:nq + no]


def local(tokens, cotangent, slot_table, w_qkv, qkv_bias, w_out, out_bias):
    dp_count = lax.axis_size("dp")
    own_index = lax.axis_index("dp")
    slot_count = slot_table.shape[0] // dp_count
    rows, width = tokens.shape
    n = math.isqrt(dp_count // 2)
    grad_scale = 1.0 / math.sqrt(dp_count * slot_count * IMG)
    slot_counts = slot_table[:, 0].reshape(dp_count, slot_count)
    own_count = lax.dynamic_index_in_dim(slot_counts, own_index, 0, keepdims=False)
    row_valid = jnp.arange(IMG)[None, :] < own_count[:, None]
    mask_rows = row_valid.reshape(rows, 1)
    local_x = tokens
    local_g = jnp.where(mask_rows, cotangent, jnp.zeros((), BF16))
    heads_here = w_out.shape[0] // HD
    full_x = lax.all_gather(local_x, "group", axis=1, tiled=True)
    full_g = lax.all_gather(local_g, "group", axis=1, tiled=True)
    projected = jnp.dot(full_x, w_qkv, preferred_element_type=F32) + qkv_bias
    projected = projected.astype(BF16).reshape(slot_count, IMG, heads_here, 3, HD)
    queries = projected[:, :, :, 0]
    key_rows = projected[:, :, :, 1]
    values = projected[:, :, :, 2]
    score_scale = 1.0 / math.sqrt(HD)
    scores = jnp.einsum("sihe,sjhe->shij", queries, key_rows, preferred_element_type=F32) * score_scale
    scores = jnp.where(row_valid[:, None, None, :], scores, -1e30)
    row_top = jnp.max(scores, axis=-1, keepdims=True)
    exponent = jnp.exp(scores - row_top)
    attn_probs = exponent / jnp.sum(exponent, axis=-1, keepdims=True)
    probs_b = attn_probs.astype(BF16)
    mixed = jnp.einsum("shij,sjhe->sihe", probs_b, values, preferred_element_type=F32)
    mixed = mixed.astype(BF16).reshape(rows, heads_here * HD)
    groups = 4
    out_parts = jnp.dot(mixed, w_out, preferred_element_type=F32).astype(BF16)
    out_parts = out_parts.reshape(rows, groups, width).transpose(1, 0, 2)
    grad_mixed = jnp.einsum("rd,cd->rc", full_g, w_out, preferred_element_type=F32)
    grad_mixed = grad_mixed.astype(BF16).reshape(slot_count, IMG, heads_here, HD)
    w_out_grad = jnp.einsum("rc,rd->cd", mixed, full_g, preferred_element_type=F32)
    out_bias_grad = jnp.sum(local_g.astype(F32), axis=0)
    grad_probs = jnp.einsum("sihe,sjhe->shij", grad_mixed, values, preferred_element_type=F32)
    inner = jnp.sum(attn_probs * grad_probs, axis=-1, keepdims=True)
    grad_scores = (attn_probs * (grad_probs - inner) * score_scale).astype(BF16)
    grad_query = jnp.einsum("shij,sjhe->sihe", grad_scores, key_rows, preferred_element_type=F32)
    grad_keys = jnp.einsum("shij,sihe->sjhe", grad_scores, queries, preferred_element_type=F32)
    grad_values = jnp.einsum("shij,sihe->sjhe", probs_b, grad_mixed, preferred_element_type=F32)
    grad_proj = jnp.stack([grad_query, grad_keys, grad_values], axis=3).reshape(rows, heads_here * 3 * HD)
    qkv_bias_grad = jnp.sum(grad_proj, axis=0)
    grad_proj_b = grad_proj.astype(BF16)
    w_qkv_grad = jnp.einsum("rd,rc->dc", full_x, grad_proj_b, preferred_element_type=F32)
    in_parts = jnp.einsum("rc,dc->rd", grad_proj_b, w_qkv, preferred_element_type=F32).astype(BF16)
    in_parts = in_parts.reshape(rows, groups, width).transpose(1, 0, 2)
    blocks = to_blocks(n, w_qkv_grad, w_out_grad, qkv_bias_grad, out_bias_grad)
    layer_out, input_grad, full = reduce_all(
        n, slot_count, grad_scale, own_count, out_parts, in_parts, blocks,
        local_x, local_g, out_bias.reshape(1, width),
    )
    d, cq = w_qkv.shape
    r2, c2 = w_out.shape
    return (layer_out, input_grad) + reorder(from_blocks(full, d, cq, r2, c2, cq, width))


def reorder(grads):
    return grads[0], grads[2], grads[1], grads[3]


def solution(mesh):
    return jax.shard_map(
        local,
        mesh=mesh,
        in_specs=(
            P("dp", "group"),
            P("dp", "group"),
            P(),
            P(None, "group"),
            P("group"),
            P("group", None),
            P("group"),
        ),
        out_specs=(
            P("dp", "group"),
            P("dp", "group"),
            P(None, "group"),
            P("group"),
            P("group", None),
            P("group"),
        ),
        check_vma=False,
    )
```

```python
import functools
import math

import jax
import jax.numpy as jnp
from jax import lax
from jax.experimental import pallas as pl
from jax.experimental.pallas import tpu as pltpu
from jax.sharding import PartitionSpec as P

HD = 80
IMG = 128
GROUPS = 4
LANES = 128
TILE = 16
MESH = pl.DeviceIdType.MESH
BF16 = jnp.bfloat16
F32 = jnp.float32


def far_first(n):
    return sorted(range(1, n), key=lambda k: (-min(k, n - k), k))


def dot(a, b):
    return jnp.dot(a, b, preferred_element_type=F32)


def dot_nt(a, b):
    return lax.dot_general(a, b, (((1,), (1,)), ((), ())), preferred_element_type=F32)


def dot_tn(a, b):
    return lax.dot_general(a, b, (((0,), (0,)), ((), ())), preferred_element_type=F32)


def kernel(
    n, nb, nb2, slots, scale,
    tab_ref, x_ref, ct_ref, wq_ref, qb_ref, wo_ref, ob_ref,
    lo_ref, ig_ref, dq_ref, dqb_ref, do_ref, dob_ref,
    gat, wos, op, ip, grad, gpf,
    r0, s1, r1, t, r2, v, full, fw, mrg, rcv,
    b0s, b0r, b1s, b1r, b2s, b2r, b3s, b3r, b4s, b4r, b5s, b5r,
    xs, xr, gs, gr_sem,
):
    width = x_ref.shape[1]
    model = width * GROUPS
    qkv = wq_ref.shape[1]
    heads = wo_ref.shape[0]
    qtiles = -(-qkv // LANES)
    otiles = -(-width // LANES)
    orow = qtiles * model
    brow = orow + otiles * GROUPS * heads
    piece_rows = nb * TILE
    part_rows = nb2 * TILE
    score_scale = 1.0 / math.sqrt(HD)

    dp = lax.axis_index("dp")
    grp = lax.axis_index("group")
    c = lax.rem(dp, 2)
    y = lax.rem(lax.div(dp, 2), n)
    z = lax.div(dp, 2 * n)
    other = dp + 1 - 2 * c
    gr = lax.rem(grp + 1, GROUPS)
    gl = lax.rem(grp + 3, GROUPS)
    gx = lax.rem(grp + 2, GROUPS)
    me = (y, z)

    def on_axis(axis, idx):
        return (z * n + idx) * 2 + c if axis == 0 else (idx * n + y) * 2 + c

    def plus(a, k):
        return lax.rem(a + k, n)

    def send(src, dst, ss, rs, d, g):
        return pltpu.make_async_remote_copy(
            src_ref=src, dst_ref=dst, send_sem=ss, recv_sem=rs,
            device_id=(d, g), device_id_type=MESH,
        )

    def rows_of(img):
        return pl.ds(pl.multiple_of(img * IMG, IMG), IMG)

    barrier = pltpu.get_barrier_semaphore()
    pl.semaphore_signal(barrier, inc=1, device_id=(other, grp), device_id_type=MESH)
    for axis in (0, 1):
        for k in range(1, n):
            pl.semaphore_signal(
                barrier, inc=1, device_id=(on_axis(axis, plus(me[axis], k)), grp),
                device_id_type=MESH,
            )
    for g in (gr, gl):
        pl.semaphore_signal(barrier, inc=1, device_id=(dp, g), device_id_type=MESH)

    def stage(img, _):
        rows = rows_of(img)
        gat[0, grp, img] = x_ref[rows]
        row = lax.broadcasted_iota(jnp.int32, (IMG, width), 0)
        keep = row < tab_ref[dp * slots + img, 0]
        gat[1, grp, img] = jnp.where(keep, ct_ref[rows].astype(F32), 0.0).astype(BF16)
        return 0

    lax.fori_loop(0, slots, stage, 0)
    half = IMG // 2
    lo_half = pl.ds(0, half)
    hi_half = pl.ds(half, half)

    def g_copy(arr, img, j):
        ch = arr * slots + img
        ref, dst = (
            (gat.at[arr, grp, img], gr),
            (gat.at[arr, grp, img], gl),
            (gat.at[arr, gl, img, lo_half], gr),
            (gat.at[arr, gr, img, hi_half], gl),
        )[j]
        return send(ref, ref, gs.at[ch, j], gr_sem.at[ch, j], dp, dst)

    def g_in(arr, img, j):
        ch = arr * slots + img
        ref = (
            gat.at[arr, gl, img],
            gat.at[arr, gr, img],
            gat.at[arr, gx, img, lo_half],
            gat.at[arr, gx, img, hi_half],
        )[j]
        return send(ref, ref, gs.at[ch, j], gr_sem.at[ch, j], dp, gr)

    def direct(img):
        for arr in (0, 1):
            for j in (0, 1):
                g_copy(arr, img, j).start()

    def forward(img):
        for arr in (0, 1):
            for j in (0, 1):
                g_in(arr, img, j).wait_recv()
                g_copy(arr, img, j + 2).start()

    pl.semaphore_wait(barrier, 1 + 2 * (n - 1) + 2)
    direct(0)
    direct(1)

    grad[...] = jnp.zeros(grad.shape, F32)
    gpf[...] = jnp.zeros(gpf.shape, F32)
    for s in range(GROUPS):
        wos[s] = wo_ref[:, s * width:(s + 1) * width]
    forward(0)

    def image(img, _):
        @pl.when(img + 2 < slots)
        def _():
            direct(img + 2)

        @pl.when(img + 1 < slots)
        def _():
            forward(img + 1)

        for arr in (0, 1):
            for j in (2, 3):
                g_in(arr, img, j).wait_recv()
        rows = rows_of(img)
        count = tab_ref[dp * slots + img, 0]
        proj = qb_ref[...]
        for s in range(GROUPS):
            proj = proj + dot(gat[0, s, img], wq_ref[s * width:(s + 1) * width, :])
        proj = proj.astype(BF16)
        gmix = dot_nt(gat[1, 0, img], wos[0])
        for s in range(1, GROUPS):
            gmix = gmix + dot_nt(gat[1, s, img], wos[s])
        gmix = gmix.astype(BF16)
        mixed = []
        for h in range(heads // HD):
            at = 3 * HD * h
            q = proj[:, at:at + HD]
            k = proj[:, at + HD:at + 2 * HD]
            val = proj[:, at + 2 * HD:at + 3 * HD]
            gm = gmix[:, h * HD:(h + 1) * HD]
            scores = dot_nt(q, k) * score_scale
            col = lax.broadcasted_iota(jnp.int32, scores.shape, 1)
            scores = jnp.where(col < count, scores, -1e30)
            ex = jnp.exp(scores - jnp.max(scores, axis=-1, keepdims=True))
            probs = ex / jnp.sum(ex, axis=-1, keepdims=True)
            probs_b = probs.astype(BF16)
            mixed.append(dot(probs_b, val).astype(BF16))
            gprobs = dot_nt(gm, val)
            inner = jnp.sum(probs * gprobs, axis=-1, keepdims=True)
            gscores = (probs * (gprobs - inner) * score_scale).astype(BF16)
            gpf[:, at:at + HD] = dot(gscores, k)
            gpf[:, at + HD:at + 2 * HD] = dot_tn(gscores, q)
            gpf[:, at + 2 * HD:at + 3 * HD] = dot_tn(probs_b, gm)
        mixed = jnp.concatenate(mixed, axis=1)
        gproj = gpf[...]
        gsum = jnp.sum(gproj, axis=0, keepdims=True)
        for j in range(qtiles):
            grad[brow + j:brow + j + 1, :] += gsum[:, j * LANES:(j + 1) * LANES]
        osum = jnp.sum(gat[1, grp, img].astype(F32), axis=0, keepdims=True)
        for j in range(otiles):
            w = min(LANES, width - j * LANES)
            at = brow + qtiles + j
            grad[at:at + 1, :w] += osum[:, j * LANES:j * LANES + w]
        gproj_b = gproj.astype(BF16)
        for s in range(GROUPS):
            op[s, rows] = dot(mixed, wos[s]).astype(BF16)
            ip[s, rows] = dot_nt(gproj_b[:, :qkv], wq_ref[s * width:(s + 1) * width, :]).astype(BF16)
            dq = dot_tn(gat[0, s, img], gproj_b)
            for j in range(qtiles):
                at = j * model + s * width
                grad[at:at + width, :] += dq[:, j * LANES:(j + 1) * LANES]
            do = dot_tn(mixed, gat[1, s, img])
            for j in range(otiles):
                w = min(LANES, width - j * LANES)
                at = orow + (j * GROUPS + s) * heads
                grad[at:at + heads, :w] += do[:, j * LANES:j * LANES + w]
        return 0

    lax.fori_loop(0, slots, image, 0)

    order = far_first(n) + [0]

    def piece(cc, s, p):
        return pl.ds(pl.multiple_of(((cc * 2 + s) * n + p) * piece_rows, TILE), piece_rows)

    def l0(s, k):
        p = plus(me[s], k)
        return send(
            grad.at[piece(1 - c, s, p)], r0.at[s, p], b0s.at[s, k], b0r.at[s, k], other, grp
        )

    for k in order:
        for s in (0, 1):
            l0(s, k).start()

    def x_copy(arr, img, j):
        src = (op, ip)[arr]
        ch = arr * slots + img
        lo = pl.ds(pl.multiple_of(img * IMG, half), half)
        hi = pl.ds(pl.multiple_of(img * IMG + half, half), half)
        ref, dst, to = (
            lambda: (src.at[gx, lo], fw.at[ch, 0], gr),
            lambda: (src.at[gx, hi], fw.at[ch, 1], gl),
            lambda: (src.at[gr, hi], rcv.at[ch, 0, 1], gr),
            lambda: (src.at[gl, lo], rcv.at[ch, 1, 0], gl),
            lambda: (mrg.at[ch, 0], rcv.at[ch, 0, 0], gr),
            lambda: (mrg.at[ch, 1], rcv.at[ch, 1, 1], gl),
        )[j]()
        return send(ref, dst, xs.at[ch, j], xr.at[ch, j], dp, to)

    for arr in (0, 1):
        def raw(img, _, arr=arr):
            for j in range(4):
                x_copy(arr, img, j).start()
            return 0
        lax.fori_loop(0, slots, raw, 0)

    def l1(s, k):
        return send(
            s1.at[s, k], r1.at[s, k], b1s.at[s, k], b1r.at[s, k],
            on_axis(s, plus(me[s], k)), grp,
        )

    for k in order:
        for s in (0, 1):
            l0(s, k).wait_recv()
            p = plus(me[s], k)
            total = grad[piece(c, s, p)] + r0[s, p]
            if k:
                s1[s, k] = total.astype(BF16)
                l1(s, k).start()
            else:
                t[s, pl.ds(0, piece_rows)] = total
                rest = part_rows * n - piece_rows
                if rest:
                    t[s, pl.ds(piece_rows, rest)] = jnp.zeros((rest, LANES), F32)

    def merge(arr):
        def step(img, _):
            ch = arr * slots + img
            src = (op, ip)[arr]
            lo = pl.ds(pl.multiple_of(img * IMG, half), half)
            hi = pl.ds(pl.multiple_of(img * IMG + half, half), half)
            x_copy(arr, img, 0).wait_recv()
            mrg[ch, 0] = (src[gr, lo].astype(F32) + fw[ch, 0].astype(F32)).astype(BF16)
            x_copy(arr, img, 4).start()
            x_copy(arr, img, 1).wait_recv()
            mrg[ch, 1] = (src[gl, hi].astype(F32) + fw[ch, 1].astype(F32)).astype(BF16)
            x_copy(arr, img, 5).start()
            return 0
        lax.fori_loop(0, slots, step, 0)

    merge(0)

    def part(q):
        return pl.ds(pl.multiple_of(q * part_rows, TILE), part_rows)

    def l2(s, k):
        q = plus(me[1 - s], k)
        return send(
            t.at[s, part(q)], r2.at[s, k], b2s.at[s, k], b2r.at[s, k], on_axis(1 - s, q), grp,
        )

    near = list(reversed(far_first(n)))
    for s in (0, 1):
        for k in near:
            l1(s, k).wait_recv()
        total = t[s, pl.ds(0, piece_rows)]
        for k in near:
            total = total + r1[s, k].astype(F32)
        t[s, pl.ds(0, piece_rows)] = total
        for k in far_first(n):
            l2(s, k).start()

    merge(1)

    def l3(s, k):
        mine = v.at[s, part(me[1 - s])]
        return send(
            mine, mine, b3s.at[s, k], b3r.at[s, k], on_axis(1 - s, plus(me[1 - s], k)), grp,
        )

    for s in (0, 1):
        for k in near:
            l2(s, k).wait_recv()
        total = t[s, part(me[1 - s])]
        for k in near:
            total = total + r2[s, k]
        v[s, part(me[1 - s])] = (total * scale).astype(BF16)
        for k in far_first(n):
            l3(s, k).start()

    def l4(s, k):
        return send(
            v.at[s, pl.ds(0, piece_rows)], full.at[piece(c, s, me[s])], b4s.at[s, k], b4r.at[s, k],
            on_axis(s, plus(me[s], k)), grp,
        )

    def l5(s, k):
        at = full.at[piece(c, s, plus(me[s], k))]
        return send(at, at, b5s.at[s, k], b5r.at[s, k], other, grp)

    def l3_in(s, k):
        at = v.at[s, part(plus(me[1 - s], n - k))]
        return send(at, at, b3s.at[s, k], b3r.at[s, k], other, grp)

    for s in (0, 1):
        for k in near:
            l3_in(s, k).wait_recv()
        for k in far_first(n):
            l4(s, k).start()
        full[piece(c, s, me[s])] = v[s, pl.ds(0, piece_rows)]
        l5(s, 0).start()

    def l4_in(s, k):
        at = full.at[piece(c, s, plus(me[s], n - k))]
        return send(at, at, b4s.at[s, k], b4r.at[s, k], other, grp)

    for k in near:
        for s in (0, 1):
            l4_in(s, k).wait_recv()
            l5(s, n - k).start()

    def finish(arr):
        def step(img, _):
            ch = arr * slots + img
            for j in range(2, 6):
                x_copy(arr, img, j).wait_recv()
            rows = rows_of(img)
            src = (op, ip)[arr]
            total = src[grp, rows].astype(F32)
            total = total + rcv[ch, 0].reshape(IMG, width).astype(F32)
            total = total + rcv[ch, 1].reshape(IMG, width).astype(F32)
            total = total + gat[arr, grp, img].astype(F32)
            if arr == 0:
                total = total + ob_ref[...]
            row = lax.broadcasted_iota(jnp.int32, total.shape, 0)
            keep = row < tab_ref[dp * slots + img, 0]
            (lo_ref, ig_ref)[arr][rows] = jnp.where(keep, total, 0.0).astype(BF16)
            return 0
        lax.fori_loop(0, slots, step, 0)

    finish(0)
    finish(1)

    def l5_in(s, k):
        at = full.at[piece(1 - c, s, plus(me[s], k))]
        return send(at, at, b5s.at[s, k], b5r.at[s, k], other, grp)

    for k in range(n):
        for s in (0, 1):
            l5_in(s, k).wait_recv()
    for j in range(qtiles):
        w = min(LANES, qkv - j * LANES)
        dq_ref[:, j * LANES:j * LANES + w] = full[j * model:(j + 1) * model, :w]
        dqb_ref[:, j * LANES:j * LANES + w] = full[brow:brow + TILE, :w].astype(F32)[j:j + 1]
    wide = []
    for s in range(GROUPS):
        for j in range(otiles):
            w = min(LANES, width - j * LANES)
            at = orow + (j * GROUPS + s) * heads
            wide.append(full[at:at + heads, :w])
    do_ref[...] = jnp.concatenate(wide, axis=1)
    for j in range(otiles):
        w = min(LANES, width - j * LANES)
        dob_ref[:, j * LANES:j * LANES + w] = (
            full[brow:brow + TILE, :w].astype(F32)[qtiles + j:qtiles + j + 1]
        )
    for k in range(n):
        for s in (0, 1):
            l0(s, k).wait_send()
            l5(s, k).wait_send()
            if k:
                l1(s, k).wait_send()
                l2(s, k).wait_send()
                l3(s, k).wait_send()
                l4(s, k).wait_send()
    for arr in (0, 1):
        def done(img, _, arr=arr):
            for j in range(6):
                x_copy(arr, img, j).wait_send()
            for j in range(4):
                g_copy(arr, img, j).wait_send()
            return 0
        lax.fori_loop(0, slots, done, 0)


def local(tokens, cotangent, slot_table, w_qkv, qkv_bias, w_out, out_bias):
    dp_count = lax.axis_size("dp")
    slots = slot_table.shape[0] // dp_count
    rows, width = tokens.shape
    model, qkv = w_qkv.shape
    heads = w_out.shape[0]
    n = math.isqrt(dp_count // 2)
    scale = 1.0 / math.sqrt(dp_count * slots * IMG)
    used = -(-qkv // LANES) * model // TILE + -(-width // LANES) * GROUPS * heads // TILE + 1
    nb = -(-used // (4 * n))
    nb2 = -(-nb // n)
    piece_rows, part_rows, half = nb * TILE, nb2 * TILE, IMG // 2
    chunks = 2 * slots
    vm = pl.BlockSpec(memory_space=pltpu.VMEM)
    dma = pltpu.SemaphoreType.DMA
    outs = pl.pallas_call(
        functools.partial(kernel, n, nb, nb2, slots, scale),
        out_shape=(
            jax.ShapeDtypeStruct((rows, width), BF16),
            jax.ShapeDtypeStruct((rows, width), BF16),
            jax.ShapeDtypeStruct((model, qkv), BF16),
            jax.ShapeDtypeStruct((1, qkv), F32),
            jax.ShapeDtypeStruct((heads, model), BF16),
            jax.ShapeDtypeStruct((1, width), F32),
        ),
        in_specs=[pl.BlockSpec(memory_space=pltpu.SMEM)] + [vm] * 6,
        out_specs=(vm,) * 6,
        scratch_shapes=[
            pltpu.VMEM((2, GROUPS, slots, IMG, width), BF16),
            pltpu.VMEM((GROUPS, heads, width), BF16),
            pltpu.VMEM((GROUPS, rows, width), BF16),
            pltpu.VMEM((GROUPS, rows, width), BF16),
            pltpu.VMEM((4 * n * piece_rows, LANES), F32),
            pltpu.VMEM((IMG, -(-qkv // LANES) * LANES), F32),
            pltpu.VMEM((2, n, piece_rows, LANES), F32),
            pltpu.VMEM((2, n, piece_rows, LANES), BF16),
            pltpu.VMEM((2, n, piece_rows, LANES), BF16),
            pltpu.VMEM((2, n * part_rows, LANES), F32),
            pltpu.VMEM((2, n, part_rows, LANES), F32),
            pltpu.VMEM((2, n * part_rows, LANES), BF16),
            pltpu.VMEM((4 * n * piece_rows, LANES), BF16),
            pltpu.VMEM((chunks, 2, half, width), BF16),
            pltpu.VMEM((chunks, 2, half, width), BF16),
            pltpu.VMEM((chunks, 2, 2, half, width), BF16),
        ] + [dma((2, n))] * 12 + [dma((chunks, 6))] * 2 + [dma((chunks, 4))] * 2,
        compiler_params=pltpu.CompilerParams(
            collective_id=0, has_side_effects=True, vmem_limit_bytes=50 * 2**20,
        ),
        cost_estimate=pl.CostEstimate(flops=4 * 10**9, bytes_accessed=10**7, transcendentals=0),
    )(slot_table, tokens, cotangent, w_qkv, qkv_bias.reshape(1, qkv), w_out, out_bias.reshape(1, width))
    layer_out, input_grad, dq, dqb, do, dob = outs
    return (layer_out, input_grad, dq, dqb.reshape(qkv), do, dob.reshape(width))


def solution(mesh):
    return jax.shard_map(
        local,
        mesh=mesh,
        in_specs=(
            P("dp", "group"),
            P("dp", "group"),
            P(),
            P(None, "group"),
            P("group"),
            P("group", None),
            P("group"),
        ),
        out_specs=(
            P("dp", "group"),
            P("dp", "group"),
            P(None, "group"),
            P("group"),
            P("group", None),
            P("group"),
        ),
        check_vma=False,
    )
```

```python
import functools
import math

import jax
import jax.numpy as jnp
from jax import lax
from jax.experimental import pallas as pl
from jax.experimental.pallas import tpu as pltpu
from jax.sharding import PartitionSpec as P

HD = 80
IMG = 128
GROUPS = 4
LANES = 128
TILE = 16
MESH = pl.DeviceIdType.MESH
BF16 = jnp.bfloat16
F32 = jnp.float32


def far_first(n):
    return sorted(range(1, n), key=lambda k: (-min(k, n - k), k))


def dot(a, b):
    return jnp.dot(a, b, preferred_element_type=F32)


def dot_nt(a, b):
    return lax.dot_general(a, b, (((1,), (1,)), ((), ())), preferred_element_type=F32)


def dot_tn(a, b):
    return lax.dot_general(a, b, (((0,), (0,)), ((), ())), preferred_element_type=F32)


def kernel(
    n, nb, nb2, slots, scale,
    tab_ref, x_ref, ct_ref, wq_ref, qb_ref, wo_ref, ob_ref,
    lo_ref, ig_ref, dq_ref, dqb_ref, do_ref, dob_ref,
    gat, ctv, wq, wqn, wo, won, qbb, obb, op, ip, grad, gpf, qsum, osum, gps, mixs,
    r0, s1, r1, t, r2, v, full, fw, mrg, rcv,
    b0s, b0r, b1s, b1r, b2s, b2r, b3s, b3r, b4s, b4r, b5s, b5r,
    xs, xr, gs, gr_sem, ls,
):
    width = x_ref.shape[0]
    model = width * GROUPS
    qkv = wq_ref.shape[0]
    heads = wo_ref.shape[0]
    both = qkv + heads
    tiles = model // LANES
    qtiles = -(-qkv // LANES)
    otiles = -(-width // LANES)
    brow = tiles * both
    piece_rows = nb * TILE
    part_rows = nb2 * TILE
    score_scale = 1.0 / math.sqrt(HD)

    dp = lax.axis_index("dp")
    grp = lax.axis_index("group")
    c = lax.rem(dp, 2)
    y = lax.rem(lax.div(dp, 2), n)
    z = lax.div(dp, 2 * n)
    other = dp + 1 - 2 * c
    gr = lax.rem(grp + 1, GROUPS)
    gl = lax.rem(grp + 3, GROUPS)
    gx = lax.rem(grp + 2, GROUPS)
    me = (y, z)

    def on_axis(axis, idx):
        return (z * n + idx) * 2 + c if axis == 0 else (idx * n + y) * 2 + c

    def plus(a, k):
        return lax.rem(a + k, n)

    def send(src, dst, ss, rs, d, g):
        return pltpu.make_async_remote_copy(
            src_ref=src, dst_ref=dst, send_sem=ss, recv_sem=rs,
            device_id=(d, g), device_id_type=MESH,
        )

    half = width // 2

    def shard(g):
        return pl.ds(pl.multiple_of(g * width, TILE), width)

    def lo_of(g):
        return pl.ds(pl.multiple_of(g * width, TILE), half)

    def hi_of(g):
        return pl.ds(pl.multiple_of(g * width + half, TILE), half)

    barrier = pltpu.get_barrier_semaphore()
    pl.semaphore_signal(barrier, inc=1, device_id=(other, grp), device_id_type=MESH)
    for axis in (0, 1):
        for k in range(1, n):
            pl.semaphore_signal(
                barrier, inc=1, device_id=(on_axis(axis, plus(me[axis], k)), grp),
                device_id_type=MESH,
            )
    for g in (gr, gl):
        pl.semaphore_signal(barrier, inc=1, device_id=(dp, g), device_id_type=MESH)

    loads = [
        pltpu.make_async_copy(
            x_ref.at[:, i * IMG:(i + 1) * IMG], gat.at[0, i, shard(grp)], ls.at[i]
        )
        for i in range(slots)
    ]
    load_ct = pltpu.make_async_copy(ct_ref, ctv, ls.at[slots])
    load_wq = pltpu.make_async_copy(wq_ref, wq, ls.at[slots + 1])
    load_wo = pltpu.make_async_copy(wo_ref, wo, ls.at[slots + 2])
    load_ct.start()
    for cp in loads:
        cp.start()
    load_wq.start()
    load_wo.start()

    def lanes_below(img, shape):
        lane = lax.broadcasted_iota(jnp.int32, shape, 1)
        return lane < tab_ref[0, dp * slots + img]

    load_ct.wait()
    for i in range(slots):
        rows = ctv[:, i * IMG:(i + 1) * IMG].astype(F32)
        gat[1, i, shard(grp)] = jnp.where(lanes_below(i, rows.shape), rows, 0.0).astype(BF16)
    for cp in loads:
        cp.wait()

    def g_copy(arr, img, j):
        ch = arr * slots + img
        at, to = (
            lambda: (shard(grp), gr),
            lambda: (shard(grp), gl),
            lambda: (lo_of(gl), gr),
            lambda: (hi_of(gr), gl),
        )[j]()
        ref = gat.at[arr, img, at]
        return send(ref, ref, gs.at[ch, j], gr_sem.at[ch, j], dp, to)

    def g_in(arr, img, j):
        ch = arr * slots + img
        at = (lambda: shard(gl), lambda: shard(gr), lambda: lo_of(gx), lambda: hi_of(gx))[j]()
        ref = gat.at[arr, img, at]
        return send(ref, ref, gs.at[ch, j], gr_sem.at[ch, j], dp, gr)

    def direct(img):
        for arr in (0, 1):
            for j in (0, 1):
                g_copy(arr, img, j).start()

    def forward(img):
        for arr in (0, 1):
            for j in (0, 1):
                g_in(arr, img, j).wait_recv()
                g_copy(arr, img, j + 2).start()

    pl.semaphore_wait(barrier, 1 + 2 * (n - 1) + 2)
    direct(0)
    direct(1)

    grad[...] = jnp.zeros(grad.shape, F32)
    qsum[...] = jnp.zeros(qsum.shape, F32)
    osum[...] = jnp.zeros(osum.shape, F32)
    qbb[...] = jnp.broadcast_to(qb_ref[...].reshape(1, qkv), (IMG, qkv)).T
    obb[...] = jnp.broadcast_to(ob_ref[...].reshape(1, width), (IMG, width)).T
    load_wq.wait()
    load_wo.wait()
    for j in range(tiles):
        wqn[j * LANES:(j + 1) * LANES] = wq[:, j * LANES:(j + 1) * LANES].T
        won[j * LANES:(j + 1) * LANES] = wo[:, j * LANES:(j + 1) * LANES].T
    forward(0)

    def image_grads(img):
        proj = (dot(wq[...], gat[0, img]) + qbb[...]).astype(BF16)
        gmix = dot(wo[...], gat[1, img]).astype(BF16)
        for h in range(heads // HD):
            at = 3 * HD * h
            q = proj[at:at + HD]
            k = proj[at + HD:at + 2 * HD]
            val = proj[at + 2 * HD:at + 3 * HD]
            gm = gmix[h * HD:(h + 1) * HD]
            scores = dot_tn(k, q) * score_scale
            row = lax.broadcasted_iota(jnp.int32, scores.shape, 0)
            scores = jnp.where(row < tab_ref[0, dp * slots + img], scores, -1e30)
            ex = jnp.exp(scores - jnp.max(scores, axis=0, keepdims=True))
            probs = ex / jnp.sum(ex, axis=0, keepdims=True)
            probs_b = probs.astype(BF16)
            mixs[h * HD:(h + 1) * HD] = dot(val, probs_b).astype(BF16)
            gprobs = dot_tn(val, gm)
            inner = jnp.sum(probs * gprobs, axis=0, keepdims=True)
            gscores = (probs * (gprobs - inner) * score_scale).astype(BF16)
            gpf[at:at + HD] = dot(k, gscores)
            gpf[at + HD:at + 2 * HD] = dot_nt(q, gscores)
            gpf[at + 2 * HD:at + 3 * HD] = dot_nt(gm, probs_b)
        gproj = gpf[...]
        qsum[...] += gproj
        osum[...] += gat[1, img, shard(grp)].astype(F32)
        gps[...] = gproj.astype(BF16)
        step = 2 * LANES
        for j in range(0, model, step):
            dq = dot_nt(gps[...], gat[0, img, j:j + step])
            do = dot_nt(mixs[...], gat[1, img, j:j + step])
            for i in range(0, step, LANES):
                at = (j + i) // LANES * both
                grad[at:at + qkv] += dq[:, i:i + LANES]
                grad[at + qkv:at + both] += do[:, i:i + LANES]

    def image_parts(img):
        op[img] = dot(won[...], mixs[...]).astype(BF16)
        ip[img] = dot(wqn[...], gps[...]).astype(BF16)

    def image(img, _):
        @pl.when(img + 2 < slots)
        def _():
            direct(img + 2)

        @pl.when(img + 1 < slots)
        def _():
            forward(img + 1)

        for arr in (0, 1):
            for j in (2, 3):
                g_in(arr, img, j).wait_recv()
        image_grads(img)

        @pl.when(img + 1 < slots)
        def _():
            image_parts(img)

        return 0

    lax.fori_loop(0, slots, image, 0)
    qtot = jnp.sum(qsum[...].T, axis=0, keepdims=True)
    otot = jnp.sum(osum[...].T, axis=0, keepdims=True)
    for j in range(qtiles):
        w = min(LANES, qkv - j * LANES)
        grad[brow + j:brow + j + 1, :w] = qtot[:, j * LANES:j * LANES + w]
    for j in range(otiles):
        w = min(LANES, width - j * LANES)
        at = brow + qtiles + j
        grad[at:at + 1, :w] = otot[:, j * LANES:j * LANES + w]

    order = far_first(n) + [0]

    def piece(cc, s, p):
        return pl.ds(pl.multiple_of(((cc * 2 + s) * n + p) * piece_rows, TILE), piece_rows)

    def l0(s, k):
        p = plus(me[s], k)
        return send(
            grad.at[piece(1 - c, s, p)], r0.at[s, p], b0s.at[s, k], b0r.at[s, k], other, grp
        )

    for k in order:
        for s in (0, 1):
            l0(s, k).start()
    image_parts(slots - 1)

    def x_copy(arr, img, j):
        src = (op, ip)[arr]
        ch = arr * slots + img
        ref, dst, to = (
            lambda: (src.at[img, lo_of(gx)], fw.at[ch, 0], gr),
            lambda: (src.at[img, hi_of(gx)], fw.at[ch, 1], gl),
            lambda: (src.at[img, hi_of(gr)], rcv.at[ch, 0, 1], gr),
            lambda: (src.at[img, lo_of(gl)], rcv.at[ch, 1, 0], gl),
            lambda: (mrg.at[ch, 0], rcv.at[ch, 0, 0], gr),
            lambda: (mrg.at[ch, 1], rcv.at[ch, 1, 1], gl),
        )[j]()
        return send(ref, dst, xs.at[ch, j], xr.at[ch, j], dp, to)

    for arr in (0, 1):
        def raw(img, _, arr=arr):
            for j in range(4):
                x_copy(arr, img, j).start()
            return 0
        lax.fori_loop(0, slots, raw, 0)

    def l1(s, k):
        return send(
            s1.at[s, k], r1.at[s, k], b1s.at[s, k], b1r.at[s, k],
            on_axis(s, plus(me[s], k)), grp,
        )

    for k in order:
        for s in (0, 1):
            l0(s, k).wait_recv()
            p = plus(me[s], k)
            total = grad[piece(c, s, p)] + r0[s, p]
            if k:
                s1[s, k] = total.astype(BF16)
                l1(s, k).start()
            else:
                t[s, pl.ds(0, piece_rows)] = total
                rest = part_rows * n - piece_rows
                if rest:
                    t[s, pl.ds(piece_rows, rest)] = jnp.zeros((rest, LANES), F32)

    def merge(arr):
        def step(img, _):
            ch = arr * slots + img
            src = (op, ip)[arr]
            x_copy(arr, img, 0).wait_recv()
            mrg[ch, 0] = (src[img, lo_of(gr)].astype(F32) + fw[ch, 0].astype(F32)).astype(BF16)
            x_copy(arr, img, 4).start()
            x_copy(arr, img, 1).wait_recv()
            mrg[ch, 1] = (src[img, hi_of(gl)].astype(F32) + fw[ch, 1].astype(F32)).astype(BF16)
            x_copy(arr, img, 5).start()
            return 0
        lax.fori_loop(0, slots, step, 0)

    merge(0)

    def part(q):
        return pl.ds(pl.multiple_of(q * part_rows, TILE), part_rows)

    def l2(s, k):
        q = plus(me[1 - s], k)
        return send(
            t.at[s, part(q)], r2.at[s, k], b2s.at[s, k], b2r.at[s, k], on_axis(1 - s, q), grp,
        )

    near = list(reversed(far_first(n)))
    for s in (0, 1):
        for k in near:
            l1(s, k).wait_recv()
        total = t[s, pl.ds(0, piece_rows)]
        for k in near:
            total = total + r1[s, k].astype(F32)
        t[s, pl.ds(0, piece_rows)] = total
        for k in far_first(n):
            l2(s, k).start()

    merge(1)

    def l3(s, k):
        mine = v.at[s, part(me[1 - s])]
        return send(
            mine, mine, b3s.at[s, k], b3r.at[s, k], on_axis(1 - s, plus(me[1 - s], k)), grp,
        )

    for s in (0, 1):
        for k in near:
            l2(s, k).wait_recv()
        total = t[s, part(me[1 - s])]
        for k in near:
            total = total + r2[s, k]
        v[s, part(me[1 - s])] = (total * scale).astype(BF16)
        for k in far_first(n):
            l3(s, k).start()

    def l4(s, k):
        return send(
            v.at[s, pl.ds(0, piece_rows)], full.at[piece(c, s, me[s])], b4s.at[s, k], b4r.at[s, k],
            on_axis(s, plus(me[s], k)), grp,
        )

    def l5(s, k):
        at = full.at[piece(c, s, plus(me[s], k))]
        return send(at, at, b5s.at[s, k], b5r.at[s, k], other, grp)

    def l3_in(s, k):
        at = v.at[s, part(plus(me[1 - s], n - k))]
        return send(at, at, b3s.at[s, k], b3r.at[s, k], other, grp)

    for s in (0, 1):
        for k in near:
            l3_in(s, k).wait_recv()
        for k in far_first(n):
            l4(s, k).start()
        full[piece(c, s, me[s])] = v[s, pl.ds(0, piece_rows)]
        l5(s, 0).start()

    def l4_in(s, k):
        at = full.at[piece(c, s, plus(me[s], n - k))]
        return send(at, at, b4s.at[s, k], b4r.at[s, k], other, grp)

    for k in near:
        for s in (0, 1):
            l4_in(s, k).wait_recv()
            l5(s, n - k).start()

    def finish(arr):
        def step(img, _):
            ch = arr * slots + img
            for j in range(2, 6):
                x_copy(arr, img, j).wait_recv()
            src = (op, ip)[arr]
            total = src[img, shard(grp)].astype(F32)
            total = total + rcv[ch, 0].reshape(width, IMG).astype(F32)
            total = total + rcv[ch, 1].reshape(width, IMG).astype(F32)
            total = total + gat[arr, img, shard(grp)].astype(F32)
            if arr == 0:
                total = total + obb[...]
            total = jnp.where(lanes_below(img, total.shape), total, 0.0).astype(BF16)
            (lo_ref, ig_ref)[arr][:, pl.ds(pl.multiple_of(img * IMG, IMG), IMG)] = total
            return 0
        lax.fori_loop(0, slots, step, 0)

    finish(0)
    finish(1)

    def l5_in(s, k):
        at = full.at[piece(1 - c, s, plus(me[s], k))]
        return send(at, at, b5s.at[s, k], b5r.at[s, k], other, grp)

    for k in range(n):
        for s in (0, 1):
            l5_in(s, k).wait_recv()
    for j in range(tiles):
        at = j * both
        dq_ref[:, j * LANES:(j + 1) * LANES] = full[at:at + qkv]
        do_ref[:, j * LANES:(j + 1) * LANES] = full[at + qkv:at + both]
    sums = full[brow:brow + TILE].astype(F32)
    for ref, size, first in ((dqb_ref, qkv, 0), (dob_ref, width, qtiles)):
        for j in range(-(-size // LANES)):
            w = min(LANES, size - j * LANES)
            ref[:, j * LANES:j * LANES + w] = sums[first + j:first + j + 1, :w]
    for k in range(n):
        for s in (0, 1):
            l0(s, k).wait_send()
            l5(s, k).wait_send()
            if k:
                l1(s, k).wait_send()
                l2(s, k).wait_send()
                l3(s, k).wait_send()
                l4(s, k).wait_send()
    for arr in (0, 1):
        def done(img, _, arr=arr):
            for j in range(6):
                x_copy(arr, img, j).wait_send()
            for j in range(4):
                g_copy(arr, img, j).wait_send()
            return 0
        lax.fori_loop(0, slots, done, 0)


def local(tokens, cotangent, slot_table, w_qkv, qkv_bias, w_out, out_bias):
    dp_count = lax.axis_size("dp")
    slots = slot_table.shape[0] // dp_count
    rows, width = tokens.shape
    model, qkv = w_qkv.shape
    heads = w_out.shape[0]
    n = math.isqrt(dp_count // 2)
    scale = 1.0 / math.sqrt(dp_count * slots * IMG)
    used = (qkv + heads) // TILE * (model // LANES) + 1
    nb = -(-used // (4 * n))
    nb2 = -(-nb // n)
    piece_rows, part_rows, half = nb * TILE, nb2 * TILE, width // 2
    chunks = 2 * slots
    vm = pl.BlockSpec(memory_space=pltpu.VMEM)
    hbm = pl.BlockSpec(memory_space=pl.ANY)
    smem = pl.BlockSpec(memory_space=pltpu.SMEM)
    dma = pltpu.SemaphoreType.DMA
    outs = pl.pallas_call(
        functools.partial(kernel, n, nb, nb2, slots, scale),
        out_shape=(
            jax.ShapeDtypeStruct((width, rows), BF16),
            jax.ShapeDtypeStruct((width, rows), BF16),
            jax.ShapeDtypeStruct((qkv, model), BF16),
            jax.ShapeDtypeStruct((1, qkv), F32),
            jax.ShapeDtypeStruct((heads, model), BF16),
            jax.ShapeDtypeStruct((1, width), F32),
        ),
        in_specs=[smem, hbm, hbm, hbm, vm, hbm, vm],
        out_specs=(vm,) * 6,
        scratch_shapes=[
            pltpu.VMEM((2, slots, model, IMG), BF16),
            pltpu.VMEM((width, rows), BF16),
            pltpu.VMEM((qkv, model), BF16),
            pltpu.VMEM((model, qkv), BF16),
            pltpu.VMEM((heads, model), BF16),
            pltpu.VMEM((model, heads), BF16),
            pltpu.VMEM((qkv, IMG), F32),
            pltpu.VMEM((width, IMG), F32),
            pltpu.VMEM((slots, model, IMG), BF16),
            pltpu.VMEM((slots, model, IMG), BF16),
            pltpu.VMEM((4 * n * piece_rows, LANES), F32),
            pltpu.VMEM((qkv, IMG), F32),
            pltpu.VMEM((qkv, IMG), F32),
            pltpu.VMEM((width, IMG), F32),
            pltpu.VMEM((qkv, IMG), BF16),
            pltpu.VMEM((heads, IMG), BF16),
            pltpu.VMEM((2, n, piece_rows, LANES), F32),
            pltpu.VMEM((2, n, piece_rows, LANES), BF16),
            pltpu.VMEM((2, n, piece_rows, LANES), BF16),
            pltpu.VMEM((2, n * part_rows, LANES), F32),
            pltpu.VMEM((2, n, part_rows, LANES), F32),
            pltpu.VMEM((2, n * part_rows, LANES), BF16),
            pltpu.VMEM((4 * n * piece_rows, LANES), BF16),
            pltpu.VMEM((chunks, 2, half, IMG), BF16),
            pltpu.VMEM((chunks, 2, half, IMG), BF16),
            pltpu.VMEM((chunks, 2, 2, half, IMG), BF16),
        ] + [dma((2, n))] * 12 + [dma((chunks, 6))] * 2 + [dma((chunks, 4))] * 2 + [dma((slots + 3,))],
        compiler_params=pltpu.CompilerParams(
            collective_id=0, has_side_effects=True, vmem_limit_bytes=50 * 2**20,
        ),
        cost_estimate=pl.CostEstimate(flops=4 * 10**9, bytes_accessed=10**7, transcendentals=0),
    )(slot_table.T, tokens.T, cotangent.T, w_qkv.T, qkv_bias.reshape(1, qkv), w_out, out_bias.reshape(1, width))
    layer_out, input_grad, dq, dqb, do, dob = outs
    return (layer_out.T, input_grad.T, dq.T, dqb.reshape(qkv), do, dob.reshape(width))


def solution(mesh):
    return jax.shard_map(
        local,
        mesh=mesh,
        in_specs=(
            P("dp", "group"),
            P("dp", "group"),
            P(),
            P(None, "group"),
            P("group"),
            P("group", None),
            P("group"),
        ),
        out_specs=(
            P("dp", "group"),
            P("dp", "group"),
            P(None, "group"),
            P("group"),
            P("group", None),
            P("group"),
        ),
        check_vma=False,
    )
```

```python
import functools
import math

import jax
import jax.numpy as jnp
from jax import lax
from jax.experimental import pallas as pl
from jax.experimental.pallas import tpu as pltpu
from jax.sharding import PartitionSpec as P

HD = 80
IMG = 128
GROUPS = 4
LANES = 128
TILE = 16
MESH = pl.DeviceIdType.MESH
BF16 = jnp.bfloat16
F32 = jnp.float32


def far_first(n):
    return sorted(range(1, n), key=lambda k: (-min(k, n - k), k))


def dot(a, b):
    return jnp.dot(a, b, preferred_element_type=F32)


def dot_nt(a, b):
    return lax.dot_general(a, b, (((1,), (1,)), ((), ())), preferred_element_type=F32)


def dot_tn(a, b):
    return lax.dot_general(a, b, (((0,), (0,)), ((), ())), preferred_element_type=F32)


def kernel(
    n, nb, nb2, slots, scale,
    tab_ref, x_ref, ct_ref, wq_ref, qb_ref, wo_ref, ob_ref,
    lo_ref, ig_ref, dq_ref, dqb_ref, do_ref, dob_ref,
    gat, ctv, tab, wq, wqn, wo, won, qb, ob, qbb, obb, op, ip, grad, gpf, qsum, osum, gps, mixs,
    r0, s1, r1, m1, t, r2, v, full, fw, mrg, rcv,
    b0s, b0r, b1s, b1r, b2s, b2r, b3s, b3r, b4s, b4r, b5s, b5r,
    xs, xr, gs, gr_sem, ls,
):
    width = x_ref.shape[0]
    model = width * GROUPS
    qkv = wq_ref.shape[0]
    heads = wo_ref.shape[0]
    both = qkv + heads
    tiles = model // LANES
    qtiles = -(-qkv // LANES)
    otiles = -(-width // LANES)
    brow = tiles * both
    piece_rows = nb * TILE
    part_rows = nb2 * TILE
    score_scale = 1.0 / math.sqrt(HD)

    dp = lax.axis_index("dp")
    grp = lax.axis_index("group")
    c = lax.rem(dp, 2)
    y = lax.rem(lax.div(dp, 2), n)
    z = lax.div(dp, 2 * n)
    other = dp + 1 - 2 * c
    gr = lax.rem(grp + 1, GROUPS)
    gl = lax.rem(grp + 3, GROUPS)
    gx = lax.rem(grp + 2, GROUPS)
    me = (y, z)

    def on_axis(axis, idx):
        return (z * n + idx) * 2 + c if axis == 0 else (idx * n + y) * 2 + c

    def plus(a, k):
        return lax.rem(a + k, n)

    def send(src, dst, ss, rs, d, g):
        return pltpu.make_async_remote_copy(
            src_ref=src, dst_ref=dst, send_sem=ss, recv_sem=rs,
            device_id=(d, g), device_id_type=MESH,
        )

    half = width // 2

    def shard(g):
        return pl.ds(pl.multiple_of(g * width, TILE), width)

    def lo_of(g):
        return pl.ds(pl.multiple_of(g * width, TILE), half)

    def hi_of(g):
        return pl.ds(pl.multiple_of(g * width + half, TILE), half)

    barrier = pltpu.get_barrier_semaphore()
    pl.semaphore_signal(barrier, inc=1, device_id=(other, grp), device_id_type=MESH)
    for axis in (0, 1):
        for k in range(1, n):
            pl.semaphore_signal(
                barrier, inc=1, device_id=(on_axis(axis, plus(me[axis], k)), grp),
                device_id_type=MESH,
            )
    for g in (gr, gl):
        pl.semaphore_signal(barrier, inc=1, device_id=(dp, g), device_id_type=MESH)

    loads = [
        pltpu.make_async_copy(
            x_ref.at[:, i * IMG:(i + 1) * IMG], gat.at[0, i, shard(grp)], ls.at[i]
        )
        for i in range(slots)
    ]
    load_ct = pltpu.make_async_copy(ct_ref, ctv, ls.at[slots])
    load_wq = pltpu.make_async_copy(wq_ref, wq, ls.at[slots + 1])
    load_wo = pltpu.make_async_copy(wo_ref, wo, ls.at[slots + 2])
    load_tab = pltpu.make_async_copy(tab_ref, tab, ls.at[slots + 3])
    load_qb = pltpu.make_async_copy(qb_ref, qb, ls.at[slots + 4])
    load_ob = pltpu.make_async_copy(ob_ref, ob, ls.at[slots + 5])
    load_tab.start()
    load_ct.start()
    for cp in loads:
        cp.start()
    load_wq.start()
    load_wo.start()
    load_qb.start()
    load_ob.start()

    def lanes_below(img, shape):
        lane = lax.broadcasted_iota(jnp.int32, shape, 1)
        return lane < tab[0, dp * slots + img]

    load_tab.wait()
    load_ct.wait()
    for i in range(slots):
        rows = ctv[:, i * IMG:(i + 1) * IMG].astype(F32)
        gat[1, i, shard(grp)] = jnp.where(lanes_below(i, rows.shape), rows, 0.0).astype(BF16)
    for cp in loads:
        cp.wait()

    def g_copy(arr, img, j):
        ch = arr * slots + img
        at, to = (
            lambda: (shard(grp), gr),
            lambda: (shard(grp), gl),
            lambda: (lo_of(gl), gr),
            lambda: (hi_of(gr), gl),
        )[j]()
        ref = gat.at[arr, img, at]
        return send(ref, ref, gs.at[ch, j], gr_sem.at[ch, j], dp, to)

    def g_in(arr, img, j):
        ch = arr * slots + img
        at = (lambda: shard(gl), lambda: shard(gr), lambda: lo_of(gx), lambda: hi_of(gx))[j]()
        ref = gat.at[arr, img, at]
        return send(ref, ref, gs.at[ch, j], gr_sem.at[ch, j], dp, gr)

    def direct(img):
        for arr in (0, 1):
            for j in (0, 1):
                g_copy(arr, img, j).start()

    def forward(img):
        for arr in (0, 1):
            for j in (0, 1):
                g_in(arr, img, j).wait_recv()
                g_copy(arr, img, j + 2).start()

    pl.semaphore_wait(barrier, 1 + 2 * (n - 1) + 2)
    direct(0)
    direct(1)

    grad[...] = jnp.zeros(grad.shape, F32)
    qsum[...] = jnp.zeros(qsum.shape, F32)
    osum[...] = jnp.zeros(osum.shape, F32)
    load_qb.wait()
    load_ob.wait()
    load_wq.wait()
    load_wo.wait()
    qbb[...] = jnp.broadcast_to(qb[...].reshape(1, qkv), (IMG, qkv)).T
    obb[...] = jnp.broadcast_to(ob[...].reshape(1, width), (IMG, width)).T
    for j in range(tiles):
        wqn[j * LANES:(j + 1) * LANES] = wq[:, j * LANES:(j + 1) * LANES].T
        won[j * LANES:(j + 1) * LANES] = wo[:, j * LANES:(j + 1) * LANES].T
    forward(0)

    def image_grads(img):
        proj = (dot(wq[...], gat[0, img]) + qbb[...]).astype(BF16)
        gmix = dot(wo[...], gat[1, img]).astype(BF16)
        for h in range(heads // HD):
            at = 3 * HD * h
            q = proj[at:at + HD]
            k = proj[at + HD:at + 2 * HD]
            val = proj[at + 2 * HD:at + 3 * HD]
            gm = gmix[h * HD:(h + 1) * HD]
            scores = dot_tn(k, q) * score_scale
            row = lax.broadcasted_iota(jnp.int32, scores.shape, 0)
            scores = jnp.where(row < tab[0, dp * slots + img], scores, -1e30)
            ex = jnp.exp(scores - jnp.max(scores, axis=0, keepdims=True))
            probs = ex / jnp.sum(ex, axis=0, keepdims=True)
            probs_b = probs.astype(BF16)
            mixs[h * HD:(h + 1) * HD] = dot(val, probs_b).astype(BF16)
            gprobs = dot_tn(val, gm)
            inner = jnp.sum(probs * gprobs, axis=0, keepdims=True)
            gscores = (probs * (gprobs - inner) * score_scale).astype(BF16)
            gpf[at:at + HD] = dot(k, gscores)
            gpf[at + HD:at + 2 * HD] = dot_nt(q, gscores)
            gpf[at + 2 * HD:at + 3 * HD] = dot_nt(gm, probs_b)
        gproj = gpf[...]
        qsum[...] += gproj
        osum[...] += gat[1, img, shard(grp)].astype(F32)
        gps[...] = gproj.astype(BF16)
        step = 2 * LANES
        for j in range(0, model, step):
            dq = dot_nt(gps[...], gat[0, img, j:j + step])
            do = dot_nt(mixs[...], gat[1, img, j:j + step])
            for i in range(0, step, LANES):
                at = (j + i) // LANES * both
                grad[at:at + qkv] += dq[:, i:i + LANES]
                grad[at + qkv:at + both] += do[:, i:i + LANES]

    def image_parts(img):
        op[img] = dot(won[...], mixs[...]).astype(BF16)
        ip[img] = dot(wqn[...], gps[...]).astype(BF16)

    def image(img, _):
        @pl.when(img + 2 < slots)
        def _():
            direct(img + 2)

        @pl.when(img + 1 < slots)
        def _():
            forward(img + 1)

        for arr in (0, 1):
            for j in (2, 3):
                g_in(arr, img, j).wait_recv()
        image_grads(img)

        @pl.when(img + 1 < slots)
        def _():
            image_parts(img)

        return 0

    lax.fori_loop(0, slots, image, 0)
    qtot = jnp.sum(qsum[...].T, axis=0, keepdims=True)
    otot = jnp.sum(osum[...].T, axis=0, keepdims=True)
    for j in range(qtiles):
        w = min(LANES, qkv - j * LANES)
        grad[brow + j:brow + j + 1, :w] = qtot[:, j * LANES:j * LANES + w]
    for j in range(otiles):
        w = min(LANES, width - j * LANES)
        at = brow + qtiles + j
        grad[at:at + 1, :w] = otot[:, j * LANES:j * LANES + w]

    order = far_first(n) + [0]

    def piece(cc, s, p):
        return pl.ds(pl.multiple_of(((cc * 2 + s) * n + p) * piece_rows, TILE), piece_rows)

    def l0(s, k):
        p = plus(me[s], k)
        return send(
            grad.at[piece(1 - c, s, p)], r0.at[s, p], b0s.at[s, k], b0r.at[s, k], other, grp
        )

    for k in order:
        for s in (0, 1):
            l0(s, k).start()
    image_parts(slots - 1)

    def x_copy(arr, img, j):
        src = (op, ip)[arr]
        ch = arr * slots + img
        ref, dst, to = (
            lambda: (src.at[img, lo_of(gx)], fw.at[ch, 0], gr),
            lambda: (src.at[img, hi_of(gx)], fw.at[ch, 1], gl),
            lambda: (src.at[img, hi_of(gr)], rcv.at[ch, 0, 1], gr),
            lambda: (src.at[img, lo_of(gl)], rcv.at[ch, 1, 0], gl),
            lambda: (mrg.at[ch, 0], rcv.at[ch, 0, 0], gr),
            lambda: (mrg.at[ch, 1], rcv.at[ch, 1, 1], gl),
        )[j]()
        return send(ref, dst, xs.at[ch, j], xr.at[ch, j], dp, to)

    for arr in (0, 1):
        def raw(img, _, arr=arr):
            for j in range(4):
                x_copy(arr, img, j).start()
            return 0
        lax.fori_loop(0, slots, raw, 0)

    tree = n == 8
    cut = nb // 2 * TILE
    head_rows, tail_rows = pl.ds(0, cut), pl.ds(cut, piece_rows - cut)

    def l1(s, k):
        ref, dst, to = s1.at[s, k], r1.at[s, k], k
        if tree and k == 3:
            to = 1
        elif tree and k == 5:
            to = 7
        elif tree and k == 4:
            ref, dst, to = s1.at[s, 4, head_rows], r1.at[s, 4, head_rows], 2
        elif tree and k == 0:
            ref, dst, to = s1.at[s, 4, tail_rows], r1.at[s, 4, tail_rows], 6
        return send(ref, dst, b1s.at[s, k], b1r.at[s, k], on_axis(s, plus(me[s], to)), grp)

    for k in order:
        for s in (0, 1):
            l0(s, k).wait_recv()
            p = plus(me[s], k)
            total = grad[piece(c, s, p)] + r0[s, p]
            if tree and k in (2, 6):
                m1[s, k // 4] = total
            elif k:
                s1[s, k] = total.astype(BF16)
                l1(s, k).start()
                if tree and k == 4:
                    l1(s, 0).start()
            else:
                t[s, pl.ds(0, piece_rows)] = total
                rest = part_rows * n - piece_rows
                if rest:
                    t[s, pl.ds(piece_rows, rest)] = jnp.zeros((rest, LANES), F32)

    def merge(arr):
        def step(img, _):
            ch = arr * slots + img
            src = (op, ip)[arr]
            x_copy(arr, img, 0).wait_recv()
            mrg[ch, 0] = (src[img, lo_of(gr)].astype(F32) + fw[ch, 0].astype(F32)).astype(BF16)
            x_copy(arr, img, 4).start()
            x_copy(arr, img, 1).wait_recv()
            mrg[ch, 1] = (src[img, hi_of(gl)].astype(F32) + fw[ch, 1].astype(F32)).astype(BF16)
            x_copy(arr, img, 5).start()
            return 0
        lax.fori_loop(0, slots, step, 0)

    if tree:
        for s in (0, 1):
            l1(s, 3).wait_recv()
            l1(s, 4).wait_recv()
            s1[s, 2, head_rows] = (
                m1[s, 0, head_rows] + r1[s, 3, head_rows].astype(F32) + r1[s, 4, head_rows].astype(F32)
            ).astype(BF16)
            s1[s, 2, tail_rows] = (m1[s, 0, tail_rows] + r1[s, 3, tail_rows].astype(F32)).astype(BF16)
            l1(s, 2).start()
            l1(s, 5).wait_recv()
            l1(s, 0).wait_recv()
            s1[s, 6, head_rows] = (m1[s, 1, head_rows] + r1[s, 5, head_rows].astype(F32)).astype(BF16)
            s1[s, 6, tail_rows] = (
                m1[s, 1, tail_rows] + r1[s, 5, tail_rows].astype(F32) + r1[s, 4, tail_rows].astype(F32)
            ).astype(BF16)
            l1(s, 6).start()

    merge(0)

    def part(q):
        return pl.ds(pl.multiple_of(q * part_rows, TILE), part_rows)

    def l2(s, k):
        q = plus(me[1 - s], k)
        return send(
            t.at[s, part(q)], r2.at[s, k], b2s.at[s, k], b2r.at[s, k], on_axis(1 - s, q), grp,
        )

    near = list(reversed(far_first(n)))
    last = [1, 7, 2, 6] if tree else near
    for s in (0, 1):
        for k in last:
            l1(s, k).wait_recv()
        total = t[s, pl.ds(0, piece_rows)]
        for k in last:
            total = total + r1[s, k].astype(F32)
        t[s, pl.ds(0, piece_rows)] = total
        for k in far_first(n):
            l2(s, k).start()

    def l3(s, k):
        mine = v.at[s, part(me[1 - s])]
        return send(
            mine, mine, b3s.at[s, k], b3r.at[s, k], on_axis(1 - s, plus(me[1 - s], k)), grp,
        )

    for s in (0, 1):
        for k in near:
            l2(s, k).wait_recv()
        total = t[s, part(me[1 - s])]
        for k in near:
            total = total + r2[s, k]
        v[s, part(me[1 - s])] = (total * scale).astype(BF16)
        for k in far_first(n):
            l3(s, k).start()

    merge(1)

    def some(cc, s, p, first, count):
        base = ((cc * 2 + s) * n + p) * piece_rows + first
        return pl.ds(pl.multiple_of(base, TILE), count)

    def l4(s, k):
        if not tree or k in (1, 2, 6, 7):
            ref, dst, to = v.at[s, pl.ds(0, piece_rows)], full.at[piece(c, s, me[s])], k
        elif k in (3, 5):
            ref = dst = full.at[piece(c, s, plus(me[s], 6 if k == 3 else 2))]
            to = 1 if k == 3 else 7
        elif k == 4:
            ref = dst = full.at[some(c, s, plus(me[s], 6), 0, cut)]
            to = 2
        else:
            ref = dst = full.at[some(c, s, plus(me[s], 2), cut, piece_rows - cut)]
            to = 6
        return send(ref, dst, b4s.at[s, k], b4r.at[s, k], on_axis(s, plus(me[s], to)), grp)

    def l5(s, k):
        at = full.at[piece(c, s, plus(me[s], k))]
        return send(at, at, b5s.at[s, k], b5r.at[s, k], other, grp)

    def l3_in(s, k):
        at = v.at[s, part(plus(me[1 - s], n - k))]
        return send(at, at, b3s.at[s, k], b3r.at[s, k], other, grp)

    for s in (0, 1):
        for k in near:
            l3_in(s, k).wait_recv()
        for k in ([2, 6, 1, 7] if tree else far_first(n)):
            l4(s, k).start()
        full[piece(c, s, me[s])] = v[s, pl.ds(0, piece_rows)]
        l5(s, 0).start()

    def l4_in(s, k):
        at = full.at[piece(c, s, plus(me[s], n - k))]
        if tree and k == 4:
            at = full.at[some(c, s, plus(me[s], 4), 0, cut)]
        elif tree and k == 0:
            at = full.at[some(c, s, plus(me[s], 4), cut, piece_rows - cut)]
        return send(at, at, b4s.at[s, k], b4r.at[s, k], other, grp)

    for k in ([2, 6, 1, 7, 3, 5, 4] if tree else near):
        for s in (0, 1):
            l4_in(s, k).wait_recv()
            if tree and k == 4:
                l4_in(s, 0).wait_recv()
            if tree and k in (2, 6):
                l4(s, 3 if k == 2 else 5).start()
                l4(s, 4 if k == 2 else 0).start()
            l5(s, n - k).start()

    def finish(arr):
        def step(img, _):
            ch = arr * slots + img
            for j in range(2, 6):
                x_copy(arr, img, j).wait_recv()
            src = (op, ip)[arr]
            total = src[img, shard(grp)].astype(F32)
            total = total + rcv[ch, 0].reshape(width, IMG).astype(F32)
            total = total + rcv[ch, 1].reshape(width, IMG).astype(F32)
            total = total + gat[arr, img, shard(grp)].astype(F32)
            if arr == 0:
                total = total + obb[...]
            total = jnp.where(lanes_below(img, total.shape), total, 0.0).astype(BF16)
            (lo_ref, ig_ref)[arr][:, pl.ds(pl.multiple_of(img * IMG, IMG), IMG)] = total
            return 0
        lax.fori_loop(0, slots, step, 0)

    finish(0)
    finish(1)

    def l5_in(s, k):
        at = full.at[piece(1 - c, s, plus(me[s], k))]
        return send(at, at, b5s.at[s, k], b5r.at[s, k], other, grp)

    for k in range(n):
        for s in (0, 1):
            l5_in(s, k).wait_recv()
    for j in range(tiles):
        at = j * both
        dq_ref[:, j * LANES:(j + 1) * LANES] = full[at:at + qkv]
        do_ref[:, j * LANES:(j + 1) * LANES] = full[at + qkv:at + both]
    sums = full[brow:brow + TILE].astype(F32)
    for ref, size, first in ((dqb_ref, qkv, 0), (dob_ref, width, qtiles)):
        for j in range(-(-size // LANES)):
            w = min(LANES, size - j * LANES)
            ref[j * LANES:j * LANES + w] = sums[first + j, :w]
    for k in range(n):
        for s in (0, 1):
            l0(s, k).wait_send()
            l5(s, k).wait_send()
            if k or tree:
                l1(s, k).wait_send()
                l4(s, k).wait_send()
            if k:
                l2(s, k).wait_send()
                l3(s, k).wait_send()
    for arr in (0, 1):
        def done(img, _, arr=arr):
            for j in range(6):
                x_copy(arr, img, j).wait_send()
            for j in range(4):
                g_copy(arr, img, j).wait_send()
            return 0
        lax.fori_loop(0, slots, done, 0)


def store_all(count, *refs):
    copies = [
        pltpu.make_async_copy(refs[i], refs[count + i], refs[-1].at[i]) for i in range(count)
    ]
    for cp in copies:
        cp.start()
    for cp in copies:
        cp.wait()


def local(tokens, cotangent, slot_table, w_qkv, qkv_bias, w_out, out_bias):
    dp_count = lax.axis_size("dp")
    slots = slot_table.shape[0] // dp_count
    rows, width = tokens.shape
    model, qkv = w_qkv.shape
    heads = w_out.shape[0]
    n = math.isqrt(dp_count // 2)
    scale = 1.0 / math.sqrt(dp_count * slots * IMG)
    used = (qkv + heads) // TILE * (model // LANES) + 1
    nb = -(-used // (4 * n))
    nb2 = -(-nb // n)
    piece_rows, part_rows, half = nb * TILE, nb2 * TILE, width // 2
    chunks = 2 * slots
    vm = pl.BlockSpec(memory_space=pltpu.VMEM)
    hbm = pl.BlockSpec(memory_space=pltpu.HBM)
    dma = pltpu.SemaphoreType.DMA
    outs = pl.pallas_call(
        functools.partial(kernel, n, nb, nb2, slots, scale),
        out_shape=(
            jax.ShapeDtypeStruct((width, rows), BF16),
            jax.ShapeDtypeStruct((width, rows), BF16),
            jax.ShapeDtypeStruct((qkv, model), BF16),
            jax.ShapeDtypeStruct((qkv,), F32),
            jax.ShapeDtypeStruct((heads, model), BF16),
            jax.ShapeDtypeStruct((width,), F32),
        ),
        in_specs=[hbm] * 7,
        out_specs=(vm,) * 6,
        scratch_shapes=[
            pltpu.VMEM((2, slots, model, IMG), BF16),
            pltpu.VMEM((width, rows), BF16),
            pltpu.SMEM(slot_table.shape[::-1], jnp.int32),
            pltpu.VMEM((qkv, model), BF16),
            pltpu.VMEM((model, qkv), BF16),
            pltpu.VMEM((heads, model), BF16),
            pltpu.VMEM((model, heads), BF16),
            pltpu.VMEM((qkv,), F32),
            pltpu.VMEM((width,), F32),
            pltpu.VMEM((qkv, IMG), F32),
            pltpu.VMEM((width, IMG), F32),
            pltpu.VMEM((slots, model, IMG), BF16),
            pltpu.VMEM((slots, model, IMG), BF16),
            pltpu.VMEM((4 * n * piece_rows, LANES), F32),
            pltpu.VMEM((qkv, IMG), F32),
            pltpu.VMEM((qkv, IMG), F32),
            pltpu.VMEM((width, IMG), F32),
            pltpu.VMEM((qkv, IMG), BF16),
            pltpu.VMEM((heads, IMG), BF16),
            pltpu.VMEM((2, n, piece_rows, LANES), F32),
            pltpu.VMEM((2, n, piece_rows, LANES), BF16),
            pltpu.VMEM((2, n, piece_rows, LANES), BF16),
            pltpu.VMEM((2, 2, piece_rows, LANES), F32),
            pltpu.VMEM((2, n * part_rows, LANES), F32),
            pltpu.VMEM((2, n, part_rows, LANES), F32),
            pltpu.VMEM((2, n * part_rows, LANES), BF16),
            pltpu.VMEM((4 * n * piece_rows, LANES), BF16),
            pltpu.VMEM((chunks, 2, half, IMG), BF16),
            pltpu.VMEM((chunks, 2, half, IMG), BF16),
            pltpu.VMEM((chunks, 2, 2, half, IMG), BF16),
        ] + [dma((2, n))] * 12 + [dma((chunks, 6))] * 2 + [dma((chunks, 4))] * 2 + [dma((slots + 6,))],
        compiler_params=pltpu.CompilerParams(
            collective_id=0, has_side_effects=True, vmem_limit_bytes=50 * 2**20,
        ),
        cost_estimate=pl.CostEstimate(flops=4 * 10**9, bytes_accessed=10**7, transcendentals=0),
    )(*(
        pltpu.with_memory_space_constraint(a, pltpu.HBM)
        for a in (slot_table.T, tokens.T, cotangent.T, w_qkv.T, qkv_bias, w_out, out_bias)
    ))
    count = len(outs)
    outs = pl.pallas_call(
        functools.partial(store_all, count),
        out_shape=tuple(jax.ShapeDtypeStruct(o.shape, o.dtype) for o in outs),
        in_specs=[vm] * count,
        out_specs=(hbm,) * count,
        scratch_shapes=[dma((count,))],
    )(*outs)
    layer_out, input_grad, dq, dqb, do, dob = outs
    return (layer_out.T, input_grad.T, dq.T, dqb, do, dob)


def solution(mesh):
    return jax.shard_map(
        local,
        mesh=mesh,
        in_specs=(
            P("dp", "group"),
            P("dp", "group"),
            P(),
            P(None, "group"),
            P("group"),
            P("group", None),
            P("group"),
        ),
        out_specs=(
            P("dp", "group"),
            P("dp", "group"),
            P(None, "group"),
            P("group"),
            P("group", None),
            P("group"),
        ),
        check_vma=False,
    )
```

```python
import functools
import math

import jax
import jax.numpy as jnp
from jax import lax
from jax.experimental import pallas as pl
from jax.experimental.pallas import tpu as pltpu
from jax.sharding import PartitionSpec as P

HD = 80
IMG = 128
GROUPS = 4
LANES = 128
TILE = 16
STREAMS = 2
AHEAD = 2
MESH = pl.DeviceIdType.MESH
BF16 = jnp.bfloat16
F32 = jnp.float32


def far_first(n):
    return sorted(range(1, n), key=lambda k: (-min(k, n - k), k))


def dot(a, b):
    return jnp.dot(a, b, preferred_element_type=F32)


def dot_nt(a, b):
    return lax.dot_general(a, b, (((1,), (1,)), ((), ())), preferred_element_type=F32)


def dot_tn(a, b):
    return lax.dot_general(a, b, (((0,), (0,)), ((), ())), preferred_element_type=F32)


def kernel(
    n, nb, nb2, slots, scale,
    tab_ref, x_ref, ct_ref, wq_ref, qb_ref, wo_ref, ob_ref,
    lo_ref, ig_ref, dq_ref, dqb_ref, do_ref, dob_ref,
    gat, ctv, tab, wq, wqn, wo, won, qb, ob, qbb, obb, op, ip, grad, gpf, qsum, osum, gps, mixs,
    r0, s1, r1, m1, t, t2, r2, v, full, fw, mrg, rcv,
    b0s, b0r, b1s, b1r, b2s, b2r, b3s, b3r, b4s, b4r, b5s, b5r,
    xs, xr, gs, gr_sem, ls,
):
    width = x_ref.shape[0]
    model = width * GROUPS
    qkv = wq_ref.shape[0]
    heads = wo_ref.shape[0]
    both = qkv + heads
    tiles = model // LANES
    qtiles = -(-qkv // LANES)
    otiles = -(-width // LANES)
    brow = tiles * both
    piece_rows = nb * TILE
    part_rows = nb2 * TILE
    score_scale = 1.0 / math.sqrt(HD)

    dp = lax.axis_index("dp")
    grp = lax.axis_index("group")
    c = lax.rem(dp, 2)
    y = lax.rem(lax.div(dp, 2), n)
    z = lax.div(dp, 2 * n)
    other = dp + 1 - 2 * c
    gr = lax.rem(grp + 1, GROUPS)
    gl = lax.rem(grp + 3, GROUPS)
    gx = lax.rem(grp + 2, GROUPS)
    me = (y, z)

    def on_axis(axis, idx):
        return (z * n + idx) * 2 + c if axis == 0 else (idx * n + y) * 2 + c

    def plus(a, k):
        return lax.rem(a + k, n)

    def send(src, dst, ss, rs, d, g):
        return pltpu.make_async_remote_copy(
            src_ref=src, dst_ref=dst, send_sem=ss, recv_sem=rs,
            device_id=(d, g), device_id_type=MESH,
        )

    half = width // 2

    def shard(g):
        return pl.ds(pl.multiple_of(g * width, TILE), width)

    def lo_of(g):
        return pl.ds(pl.multiple_of(g * width, TILE), half)

    def hi_of(g):
        return pl.ds(pl.multiple_of(g * width + half, TILE), half)

    loads = [
        pltpu.make_async_copy(
            x_ref.at[:, i * IMG:(i + 1) * IMG], gat.at[0, i, shard(grp)], ls.at[i]
        )
        for i in range(slots)
    ]
    load_ct = pltpu.make_async_copy(ct_ref, ctv, ls.at[slots])
    load_wq = pltpu.make_async_copy(wq_ref, wq, ls.at[slots + 1])
    load_wo = pltpu.make_async_copy(wo_ref, wo, ls.at[slots + 2])
    load_tab = pltpu.make_async_copy(tab_ref, tab, ls.at[slots + 3])
    load_qb = pltpu.make_async_copy(qb_ref, qb, ls.at[slots + 4])
    load_ob = pltpu.make_async_copy(ob_ref, ob, ls.at[slots + 5])
    loads[0].start()
    load_tab.start()
    load_ct.start()

    barrier = pltpu.get_barrier_semaphore()
    for g in (gr, gl):
        pl.semaphore_signal(barrier, inc=1, device_id=(dp, g), device_id_type=MESH)
    pl.semaphore_signal(barrier, inc=1, device_id=(other, grp), device_id_type=MESH)
    for axis in (0, 1):
        for k in range(1, n):
            pl.semaphore_signal(
                barrier, inc=1, device_id=(on_axis(axis, plus(me[axis], k)), grp),
                device_id_type=MESH,
            )

    for cp in loads[1:]:
        cp.start()
    load_wq.start()
    load_wo.start()
    load_qb.start()
    load_ob.start()

    def lanes_below(img, shape):
        lane = lax.broadcasted_iota(jnp.int32, shape, 1)
        return lane < tab[0, dp * slots + img]

    def mask(i):
        rows = ctv[:, i * IMG:(i + 1) * IMG].astype(F32)
        gat[1, i, shard(grp)] = jnp.where(lanes_below(i, rows.shape), rows, 0.0).astype(BF16)

    def g_copy(arr, img, j):
        ch = arr * slots + img
        at, to = (
            lambda: (shard(grp), gr),
            lambda: (shard(grp), gl),
            lambda: (lo_of(gl), gr),
            lambda: (hi_of(gr), gl),
        )[j]()
        ref = gat.at[arr, img, at]
        return send(ref, ref, gs.at[ch, j], gr_sem.at[ch, j], dp, to)

    def g_in(arr, img, j):
        ch = arr * slots + img
        at = (lambda: shard(gl), lambda: shard(gr), lambda: lo_of(gx), lambda: hi_of(gx))[j]()
        ref = gat.at[arr, img, at]
        return send(ref, ref, gs.at[ch, j], gr_sem.at[ch, j], dp, gr)

    def direct(img, arrs=(0, 1)):
        for arr in arrs:
            for j in (0, 1):
                g_copy(arr, img, j).start()

    def forward(img):
        for arr in (0, 1):
            for j in (0, 1):
                g_in(arr, img, j).wait_recv()
                g_copy(arr, img, j + 2).start()

    pl.semaphore_wait(barrier, 1 + 2 * (n - 1) + 2)
    loads[0].wait()
    direct(0, (0,))
    load_tab.wait()
    load_ct.wait()
    mask(0)
    direct(0, (1,))
    for i in range(1, slots):
        loads[i].wait()
        mask(i)
        if i < AHEAD:
            direct(i)

    grad[...] = jnp.zeros(grad.shape, F32)
    qsum[...] = jnp.zeros(qsum.shape, F32)
    osum[...] = jnp.zeros(osum.shape, F32)
    load_qb.wait()
    load_ob.wait()
    load_wq.wait()
    load_wo.wait()
    qbb[...] = jnp.broadcast_to(qb[...].reshape(1, qkv), (IMG, qkv)).T
    obb[...] = jnp.broadcast_to(ob[...].reshape(1, width), (IMG, width)).T
    for j in range(tiles):
        wqn[j * LANES:(j + 1) * LANES] = wq[:, j * LANES:(j + 1) * LANES].T
        won[j * LANES:(j + 1) * LANES] = wo[:, j * LANES:(j + 1) * LANES].T
    forward(0)

    def halves_in(arr, img):
        for j in (2, 3):
            g_in(arr, img, j).wait_recv()

    def image_grads(img):
        halves_in(0, img)
        halves_in(1, img)
        proj = (dot(wq[...], gat[0, img]) + qbb[...]).astype(BF16)
        gmix = dot(wo[...], gat[1, img]).astype(BF16)
        for h in range(heads // HD):
            at = 3 * HD * h
            q = proj[at:at + HD]
            k = proj[at + HD:at + 2 * HD]
            val = proj[at + 2 * HD:at + 3 * HD]
            scores = dot_tn(k, q) * score_scale
            row = lax.broadcasted_iota(jnp.int32, scores.shape, 0)
            scores = jnp.where(row < tab[0, dp * slots + img], scores, -1e30)
            ex = jnp.exp(scores - jnp.max(scores, axis=0, keepdims=True))
            probs = ex / jnp.sum(ex, axis=0, keepdims=True)
            probs_b = probs.astype(BF16)
            mixs[h * HD:(h + 1) * HD] = dot(val, probs_b).astype(BF16)
            gm = gmix[h * HD:(h + 1) * HD]
            gprobs = dot_tn(val, gm)
            inner = jnp.sum(probs * gprobs, axis=0, keepdims=True)
            gscores = (probs * (gprobs - inner) * score_scale).astype(BF16)
            gpf[at:at + HD] = dot(k, gscores)
            gpf[at + HD:at + 2 * HD] = dot_nt(q, gscores)
            gpf[at + 2 * HD:at + 3 * HD] = dot_nt(gm, probs_b)
        gproj = gpf[...]
        qsum[...] += gproj
        osum[...] += gat[1, img, shard(grp)].astype(F32)
        gps[...] = gproj.astype(BF16)
        step = 2 * LANES
        for j in range(0, model, step):
            dq = dot_nt(gps[...], gat[0, img, j:j + step])
            do = dot_nt(mixs[...], gat[1, img, j:j + step])
            for i in range(0, step, LANES):
                at = (j + i) // LANES * both
                grad[at:at + qkv] += dq[:, i:i + LANES]
                grad[at + qkv:at + both] += do[:, i:i + LANES]

    def image_parts(img):
        op[img] = dot(won[...], mixs[...]).astype(BF16)
        ip[img] = dot(wqn[...], gps[...]).astype(BF16)

    def image(img, _):
        @pl.when(img + AHEAD < slots)
        def _():
            direct(img + AHEAD)

        @pl.when(img + 1 < slots)
        def _():
            forward(img + 1)

        image_grads(img)

        @pl.when(img + 1 < slots)
        def _():
            image_parts(img)

        return 0

    lax.fori_loop(0, slots, image, 0)
    qtot = jnp.sum(qsum[...].T, axis=0, keepdims=True)
    otot = jnp.sum(osum[...].T, axis=0, keepdims=True)
    for j in range(qtiles):
        w = min(LANES, qkv - j * LANES)
        grad[brow + j:brow + j + 1, :w] = qtot[:, j * LANES:j * LANES + w]
    for j in range(otiles):
        w = min(LANES, width - j * LANES)
        at = brow + qtiles + j
        grad[at:at + 1, :w] = otot[:, j * LANES:j * LANES + w]

    order = far_first(n) + [0]

    def piece(cc, s, p):
        return pl.ds(pl.multiple_of(((cc * STREAMS + s) * n + p) * piece_rows, TILE), piece_rows)

    def l0(s, k):
        p = plus(me[s % 2], k)
        return send(
            grad.at[piece(1 - c, s, p)], r0.at[s, p], b0s.at[s, k], b0r.at[s, k], other, grp
        )

    for k in order:
        for s in range(STREAMS):
            l0(s, k).start()
    image_parts(slots - 1)

    def x_copy(arr, img, j):
        src = (op, ip)[arr]
        ch = arr * slots + img
        ref, dst, to = (
            lambda: (src.at[img, lo_of(gx)], fw.at[ch, 0], gr),
            lambda: (src.at[img, hi_of(gx)], fw.at[ch, 1], gl),
            lambda: (src.at[img, hi_of(gr)], rcv.at[ch, 0, 1], gr),
            lambda: (src.at[img, lo_of(gl)], rcv.at[ch, 1, 0], gl),
            lambda: (mrg.at[ch, 0], rcv.at[ch, 0, 0], gr),
            lambda: (mrg.at[ch, 1], rcv.at[ch, 1, 1], gl),
        )[j]()
        return send(ref, dst, xs.at[ch, j], xr.at[ch, j], dp, to)

    def merge(arr):
        def step(img, _):
            ch = arr * slots + img
            src = (op, ip)[arr]
            x_copy(arr, img, 0).wait_recv()
            mrg[ch, 0] = (src[img, lo_of(gr)].astype(F32) + fw[ch, 0].astype(F32)).astype(BF16)
            x_copy(arr, img, 4).start()
            x_copy(arr, img, 1).wait_recv()
            mrg[ch, 1] = (src[img, hi_of(gl)].astype(F32) + fw[ch, 1].astype(F32)).astype(BF16)
            x_copy(arr, img, 5).start()
            return 0
        lax.fori_loop(0, slots, step, 0)

    for arr in (0, 1):
        def raw(img, _, arr=arr):
            for j in range(4):
                x_copy(arr, img, j).start()
            return 0
        lax.fori_loop(0, slots, raw, 0)

    tree = n == 8
    cut = nb // 2 * TILE
    head_rows, tail_rows = pl.ds(0, cut), pl.ds(cut, piece_rows - cut)

    def l1(s, k):
        ref, dst, to = s1.at[s, k], r1.at[s, k], k
        if tree and k == 3:
            to = 1
        elif tree and k == 5:
            to = 7
        elif tree and k == 4:
            ref, dst, to = s1.at[s, 4, head_rows], r1.at[s, 4, head_rows], 2
        elif tree and k == 0:
            ref, dst, to = s1.at[s, 4, tail_rows], r1.at[s, 4, tail_rows], 6
        return send(ref, dst, b1s.at[s, k], b1r.at[s, k], on_axis(s % 2, plus(me[s % 2], to)), grp)

    for k in order:
        for s in range(STREAMS):
            l0(s, k).wait_recv()
            p = plus(me[s % 2], k)
            total = grad[piece(c, s, p)] + r0[s, p]
            if tree and k in (2, 6):
                m1[s, k // 4] = total
            elif k:
                s1[s, k] = total.astype(BF16)
                l1(s, k).start()
                if tree and k == 4:
                    l1(s, 0).start()
            else:
                t[s, pl.ds(0, piece_rows)] = total
                rest = part_rows * n - piece_rows
                if rest:
                    t[s, pl.ds(piece_rows, rest)] = jnp.zeros((rest, LANES), F32)
                    t2[s, pl.ds(piece_rows, rest)] = jnp.zeros((rest, LANES), BF16)

    if tree:
        for s in range(STREAMS):
            l1(s, 3).wait_recv()
            l1(s, 4).wait_recv()
            s1[s, 2, head_rows] = (
                m1[s, 0, head_rows] + r1[s, 3, head_rows].astype(F32) + r1[s, 4, head_rows].astype(F32)
            ).astype(BF16)
            s1[s, 2, tail_rows] = (m1[s, 0, tail_rows] + r1[s, 3, tail_rows].astype(F32)).astype(BF16)
            l1(s, 2).start()
            l1(s, 5).wait_recv()
            l1(s, 0).wait_recv()
            s1[s, 6, head_rows] = (m1[s, 1, head_rows] + r1[s, 5, head_rows].astype(F32)).astype(BF16)
            s1[s, 6, tail_rows] = (
                m1[s, 1, tail_rows] + r1[s, 5, tail_rows].astype(F32) + r1[s, 4, tail_rows].astype(F32)
            ).astype(BF16)
            l1(s, 6).start()

    def part(q):
        return pl.ds(pl.multiple_of(q * part_rows, TILE), part_rows)

    def l2(s, k):
        q = plus(me[1 - s % 2], k)
        return send(
            t2.at[s, part(q)], r2.at[s, k], b2s.at[s, k], b2r.at[s, k], on_axis(1 - s % 2, q), grp,
        )

    near = list(reversed(far_first(n)))
    last = [1, 7, 2, 6] if tree else near
    for s in range(STREAMS):
        for k in last:
            l1(s, k).wait_recv()
        total = t[s, pl.ds(0, piece_rows)]
        for k in last:
            total = total + r1[s, k].astype(F32)
        t[s, pl.ds(0, piece_rows)] = total
        t2[s, pl.ds(0, piece_rows)] = total.astype(BF16)
        for k in far_first(n):
            l2(s, k).start()

    def l3(s, k):
        mine = v.at[s, part(me[1 - s % 2])]
        return send(
            mine, mine, b3s.at[s, k], b3r.at[s, k], on_axis(1 - s % 2, plus(me[1 - s % 2], k)), grp,
        )

    for s in range(STREAMS):
        for k in near:
            l2(s, k).wait_recv()
        total = t[s, part(me[1 - s % 2])]
        for k in near:
            total = total + r2[s, k].astype(F32)
        v[s, part(me[1 - s % 2])] = (total * scale).astype(BF16)
        for k in far_first(n):
            l3(s, k).start()

    merge(0)

    def some(cc, s, p, first, count):
        base = ((cc * STREAMS + s) * n + p) * piece_rows + first
        return pl.ds(pl.multiple_of(base, TILE), count)

    def l4(s, k):
        if not tree or k in (1, 2, 6, 7):
            ref, dst, to = v.at[s, pl.ds(0, piece_rows)], full.at[piece(c, s, me[s % 2])], k
        elif k in (3, 5):
            ref = dst = full.at[piece(c, s, plus(me[s % 2], 6 if k == 3 else 2))]
            to = 1 if k == 3 else 7
        elif k == 4:
            ref = dst = full.at[some(c, s, plus(me[s % 2], 6), 0, cut)]
            to = 2
        else:
            ref = dst = full.at[some(c, s, plus(me[s % 2], 2), cut, piece_rows - cut)]
            to = 6
        return send(ref, dst, b4s.at[s, k], b4r.at[s, k], on_axis(s % 2, plus(me[s % 2], to)), grp)

    def l5(s, k):
        at = full.at[piece(c, s, plus(me[s % 2], k))]
        return send(at, at, b5s.at[s, k], b5r.at[s, k], other, grp)

    def l3_in(s, k):
        at = v.at[s, part(plus(me[1 - s % 2], n - k))]
        return send(at, at, b3s.at[s, k], b3r.at[s, k], other, grp)

    for s in range(STREAMS):
        for k in near:
            l3_in(s, k).wait_recv()
        for k in ([2, 6, 1, 7] if tree else far_first(n)):
            l4(s, k).start()
        full[piece(c, s, me[s % 2])] = v[s, pl.ds(0, piece_rows)]
        l5(s, 0).start()

    merge(1)

    def l4_in(s, k):
        at = full.at[piece(c, s, plus(me[s % 2], n - k))]
        if tree and k == 4:
            at = full.at[some(c, s, plus(me[s % 2], 4), 0, cut)]
        elif tree and k == 0:
            at = full.at[some(c, s, plus(me[s % 2], 4), cut, piece_rows - cut)]
        return send(at, at, b4s.at[s, k], b4r.at[s, k], other, grp)

    for k in ([2, 6, 1, 7, 3, 5, 4] if tree else near):
        for s in range(STREAMS):
            l4_in(s, k).wait_recv()
            if tree and k == 4:
                l4_in(s, 0).wait_recv()
            if tree and k in (2, 6):
                l4(s, 3 if k == 2 else 5).start()
                l4(s, 4 if k == 2 else 0).start()
            l5(s, n - k).start()

    def finish(arr):
        def step(img, _):
            ch = arr * slots + img
            for j in range(2, 6):
                x_copy(arr, img, j).wait_recv()
            src = (op, ip)[arr]
            total = src[img, shard(grp)].astype(F32)
            total = total + rcv[ch, 0].reshape(width, IMG).astype(F32)
            total = total + rcv[ch, 1].reshape(width, IMG).astype(F32)
            total = total + gat[arr, img, shard(grp)].astype(F32)
            if arr == 0:
                total = total + obb[...]
            total = jnp.where(lanes_below(img, total.shape), total, 0.0).astype(BF16)
            (lo_ref, ig_ref)[arr][:, pl.ds(pl.multiple_of(img * IMG, IMG), IMG)] = total
            return 0
        lax.fori_loop(0, slots, step, 0)

    finish(0)
    finish(1)

    def l5_in(s, k):
        at = full.at[piece(1 - c, s, plus(me[s % 2], k))]
        return send(at, at, b5s.at[s, k], b5r.at[s, k], other, grp)

    for k in range(n):
        for s in range(STREAMS):
            l5_in(s, k).wait_recv()
    for j in range(tiles):
        at = j * both
        dq_ref[:, j * LANES:(j + 1) * LANES] = full[at:at + qkv]
        do_ref[:, j * LANES:(j + 1) * LANES] = full[at + qkv:at + both]
    sums = full[brow:brow + TILE].astype(F32)
    for ref, size, first in ((dqb_ref, qkv, 0), (dob_ref, width, qtiles)):
        for j in range(-(-size // LANES)):
            w = min(LANES, size - j * LANES)
            ref[j * LANES:j * LANES + w] = sums[first + j, :w]
    for k in range(n):
        for s in range(STREAMS):
            l0(s, k).wait_send()
            l5(s, k).wait_send()
            if k or tree:
                l1(s, k).wait_send()
                l4(s, k).wait_send()
            if k:
                l2(s, k).wait_send()
                l3(s, k).wait_send()
    for arr in (0, 1):
        def done(img, _, arr=arr):
            for j in range(6):
                x_copy(arr, img, j).wait_send()
            for j in range(4):
                g_copy(arr, img, j).wait_send()
            return 0
        lax.fori_loop(0, slots, done, 0)


def store_all(count, *refs):
    copies = [
        pltpu.make_async_copy(refs[i], refs[count + i], refs[-1].at[i]) for i in range(count)
    ]
    for cp in copies:
        cp.start()
    for cp in copies:
        cp.wait()


def local(tokens, cotangent, slot_table, w_qkv, qkv_bias, w_out, out_bias):
    dp_count = lax.axis_size("dp")
    slots = slot_table.shape[0] // dp_count
    rows, width = tokens.shape
    model, qkv = w_qkv.shape
    heads = w_out.shape[0]
    n = math.isqrt(dp_count // 2)
    scale = 1.0 / math.sqrt(dp_count * slots * IMG)
    used = (qkv + heads) // TILE * (model // LANES) + 1
    nb = -(-used // (2 * STREAMS * n))
    nb2 = -(-nb // n)
    piece_rows, part_rows, half = nb * TILE, nb2 * TILE, width // 2
    chunks = 2 * slots
    vm = pl.BlockSpec(memory_space=pltpu.VMEM)
    hbm = pl.BlockSpec(memory_space=pltpu.HBM)
    dma = pltpu.SemaphoreType.DMA
    outs = pl.pallas_call(
        functools.partial(kernel, n, nb, nb2, slots, scale),
        out_shape=(
            jax.ShapeDtypeStruct((width, rows), BF16),
            jax.ShapeDtypeStruct((width, rows), BF16),
            jax.ShapeDtypeStruct((qkv, model), BF16),
            jax.ShapeDtypeStruct((qkv,), F32),
            jax.ShapeDtypeStruct((heads, model), BF16),
            jax.ShapeDtypeStruct((width,), F32),
        ),
        in_specs=[hbm] * 7,
        out_specs=(vm,) * 6,
        scratch_shapes=[
            pltpu.VMEM((2, slots, model, IMG), BF16),
            pltpu.VMEM((width, rows), BF16),
            pltpu.SMEM(slot_table.shape[::-1], jnp.int32),
            pltpu.VMEM((qkv, model), BF16),
            pltpu.VMEM((model, qkv), BF16),
            pltpu.VMEM((heads, model), BF16),
            pltpu.VMEM((model, heads), BF16),
            pltpu.VMEM((qkv,), F32),
            pltpu.VMEM((width,), F32),
            pltpu.VMEM((qkv, IMG), F32),
            pltpu.VMEM((width, IMG), F32),
            pltpu.VMEM((slots, model, IMG), BF16),
            pltpu.VMEM((slots, model, IMG), BF16),
            pltpu.VMEM((2 * STREAMS * n * piece_rows, LANES), F32),
            pltpu.VMEM((qkv, IMG), F32),
            pltpu.VMEM((qkv, IMG), F32),
            pltpu.VMEM((width, IMG), F32),
            pltpu.VMEM((qkv, IMG), BF16),
            pltpu.VMEM((heads, IMG), BF16),
            pltpu.VMEM((STREAMS, n, piece_rows, LANES), F32),
            pltpu.VMEM((STREAMS, n, piece_rows, LANES), BF16),
            pltpu.VMEM((STREAMS, n, piece_rows, LANES), BF16),
            pltpu.VMEM((STREAMS, 2, piece_rows, LANES), F32),
            pltpu.VMEM((STREAMS, n * part_rows, LANES), F32),
            pltpu.VMEM((STREAMS, n * part_rows, LANES), BF16),
            pltpu.VMEM((STREAMS, n, part_rows, LANES), BF16),
            pltpu.VMEM((STREAMS, n * part_rows, LANES), BF16),
            pltpu.VMEM((2 * STREAMS * n * piece_rows, LANES), BF16),
            pltpu.VMEM((chunks, 2, half, IMG), BF16),
            pltpu.VMEM((chunks, 2, half, IMG), BF16),
            pltpu.VMEM((chunks, 2, 2, half, IMG), BF16),
        ] + [dma((STREAMS, n))] * 12 + [dma((chunks, 6))] * 2 + [dma((chunks, 4))] * 2 + [dma((slots + 6,))],
        compiler_params=pltpu.CompilerParams(
            collective_id=0, has_side_effects=True, vmem_limit_bytes=50 * 2**20,
        ),
        cost_estimate=pl.CostEstimate(flops=4 * 10**9, bytes_accessed=10**7, transcendentals=0),
    )(*(
        pltpu.with_memory_space_constraint(a, pltpu.HBM)
        for a in (slot_table.T, tokens.T, cotangent.T, w_qkv.T, qkv_bias, w_out, out_bias)
    ))
    count = len(outs)
    outs = pl.pallas_call(
        functools.partial(store_all, count),
        out_shape=tuple(jax.ShapeDtypeStruct(o.shape, o.dtype) for o in outs),
        in_specs=[vm] * count,
        out_specs=(hbm,) * count,
        scratch_shapes=[dma((count,))],
        compiler_params=pltpu.CompilerParams(vmem_limit_bytes=8 * 2**20),
    )(*(pltpu.with_memory_space_constraint(o, pltpu.VMEM) for o in outs))
    layer_out, input_grad, dq, dqb, do, dob = outs
    return (layer_out.T, input_grad.T, dq.T, dqb, do, dob)


def solution(mesh):
    return jax.shard_map(
        local,
        mesh=mesh,
        in_specs=(
            P("dp", "group"),
            P("dp", "group"),
            P(),
            P(None, "group"),
            P("group"),
            P("group", None),
            P("group"),
        ),
        out_specs=(
            P("dp", "group"),
            P("dp", "group"),
            P(None, "group"),
            P("group"),
            P("group", None),
            P("group"),
        ),
        check_vma=False,
    )
```

```python
import functools
import math

import jax
import jax.numpy as jnp
from jax import lax
from jax.experimental import pallas as pl
from jax.experimental.pallas import tpu as pltpu
from jax.sharding import PartitionSpec as P

HD = 80
IMG = 128
GROUPS = 4
LANES = 128
TILE = 16
STREAMS = 2
AHEAD = 2
MESH = pl.DeviceIdType.MESH
BF16 = jnp.bfloat16
F32 = jnp.float32


def far_first(n):
    return sorted(range(1, n), key=lambda k: (-min(k, n - k), k))


def dot(a, b):
    return jnp.dot(a, b, preferred_element_type=F32)


def dot_nt(a, b):
    return lax.dot_general(a, b, (((1,), (1,)), ((), ())), preferred_element_type=F32)


def dot_tn(a, b):
    return lax.dot_general(a, b, (((0,), (0,)), ((), ())), preferred_element_type=F32)


def kernel(
    n, nb, nb2, slots, scale,
    tab_ref, x_ref, ct_ref, wq_ref, qb_ref, wo_ref, ob_ref,
    lo_ref, ig_ref, dq_ref, dqb_ref, do_ref, dob_ref,
    gat, ctv, tab, wq, wqn, wo, won, qb, ob, qbb, obb, op, ip, grad, gpf, qsum, osum, gps, mixs,
    r0, s1, r1, m1, t, r2, v, full, fw, mrg, rcv,
    b0s, b0r, b1s, b1r, b2s, b2r, b3s, b3r, b4s, b4r, b5s, b5r,
    xs, xr, gs, gr_sem, ls,
):
    width = x_ref.shape[0]
    model = width * GROUPS
    qkv = wq_ref.shape[0]
    heads = wo_ref.shape[0]
    both = qkv + heads
    tiles = model // LANES
    qtiles = -(-qkv // LANES)
    otiles = -(-width // LANES)
    brow = tiles * both
    piece_rows = nb * TILE
    part_rows = nb2 * TILE
    score_scale = 1.0 / math.sqrt(HD)

    dp = lax.axis_index("dp")
    grp = lax.axis_index("group")
    c = lax.rem(dp, 2)
    y = lax.rem(lax.div(dp, 2), n)
    z = lax.div(dp, 2 * n)
    other = dp + 1 - 2 * c
    gr = lax.rem(grp + 1, GROUPS)
    gl = lax.rem(grp + 3, GROUPS)
    gx = lax.rem(grp + 2, GROUPS)
    me = (y, z)

    def on_axis(axis, idx):
        return (z * n + idx) * 2 + c if axis == 0 else (idx * n + y) * 2 + c

    def plus(a, k):
        return lax.rem(a + k, n)

    def send(src, dst, ss, rs, d, g):
        return pltpu.make_async_remote_copy(
            src_ref=src, dst_ref=dst, send_sem=ss, recv_sem=rs,
            device_id=(d, g), device_id_type=MESH,
        )

    half = width // 2

    def shard(g):
        return pl.ds(pl.multiple_of(g * width, TILE), width)

    def lo_of(g):
        return pl.ds(pl.multiple_of(g * width, TILE), half)

    def hi_of(g):
        return pl.ds(pl.multiple_of(g * width + half, TILE), half)

    loads = [
        pltpu.make_async_copy(
            x_ref.at[:, i * IMG:(i + 1) * IMG], gat.at[0, i, shard(grp)], ls.at[i]
        )
        for i in range(slots)
    ]
    load_ct = pltpu.make_async_copy(ct_ref, ctv, ls.at[slots])
    load_wq = pltpu.make_async_copy(wq_ref, wq, ls.at[slots + 1])
    load_wo = pltpu.make_async_copy(wo_ref, wo, ls.at[slots + 2])
    load_tab = pltpu.make_async_copy(tab_ref, tab, ls.at[slots + 3])
    load_qb = pltpu.make_async_copy(qb_ref, qb, ls.at[slots + 4])
    load_ob = pltpu.make_async_copy(ob_ref, ob, ls.at[slots + 5])
    loads[0].start()
    load_tab.start()
    load_ct.start()

    barrier = pltpu.get_barrier_semaphore()
    for g in (gr, gl):
        pl.semaphore_signal(barrier, inc=1, device_id=(dp, g), device_id_type=MESH)
    pl.semaphore_signal(barrier, inc=1, device_id=(other, grp), device_id_type=MESH)
    for axis in (0, 1):
        for k in range(1, n):
            pl.semaphore_signal(
                barrier, inc=1, device_id=(on_axis(axis, plus(me[axis], k)), grp),
                device_id_type=MESH,
            )

    for cp in loads[1:]:
        cp.start()
    load_wq.start()
    load_wo.start()
    load_qb.start()
    load_ob.start()

    def lanes_below(img, shape):
        lane = lax.broadcasted_iota(jnp.int32, shape, 1)
        return lane < tab[0, dp * slots + img]

    def mask(i):
        rows = ctv[:, i * IMG:(i + 1) * IMG].astype(F32)
        gat[1, i, shard(grp)] = jnp.where(lanes_below(i, rows.shape), rows, 0.0).astype(BF16)

    def g_copy(arr, img, j):
        ch = arr * slots + img
        at, to = (
            lambda: (shard(grp), gr),
            lambda: (shard(grp), gl),
            lambda: (lo_of(gl), gr),
            lambda: (hi_of(gr), gl),
        )[j]()
        ref = gat.at[arr, img, at]
        return send(ref, ref, gs.at[ch, j], gr_sem.at[ch, j], dp, to)

    def g_in(arr, img, j):
        ch = arr * slots + img
        at = (lambda: shard(gl), lambda: shard(gr), lambda: lo_of(gx), lambda: hi_of(gx))[j]()
        ref = gat.at[arr, img, at]
        return send(ref, ref, gs.at[ch, j], gr_sem.at[ch, j], dp, gr)

    def direct(img, arrs=(0, 1)):
        for arr in arrs:
            for j in (0, 1):
                g_copy(arr, img, j).start()

    def forward(img):
        for arr in (0, 1):
            for j in (0, 1):
                g_in(arr, img, j).wait_recv()
                g_copy(arr, img, j + 2).start()

    pl.semaphore_wait(barrier, 1 + 2 * (n - 1) + 2)
    loads[0].wait()
    direct(0, (0,))
    load_tab.wait()
    load_ct.wait()
    mask(0)
    direct(0, (1,))
    for i in range(1, slots):
        loads[i].wait()
        mask(i)
        if i < AHEAD:
            direct(i)

    grad[...] = jnp.zeros(grad.shape, F32)
    qsum[...] = jnp.zeros(qsum.shape, F32)
    osum[...] = jnp.zeros(osum.shape, F32)
    load_qb.wait()
    load_ob.wait()
    load_wq.wait()
    load_wo.wait()
    qbb[...] = jnp.broadcast_to(qb[...].reshape(1, qkv), (IMG, qkv)).T
    obb[...] = jnp.broadcast_to(ob[...].reshape(1, width), (IMG, width)).T
    for j in range(tiles):
        wqn[j * LANES:(j + 1) * LANES] = wq[:, j * LANES:(j + 1) * LANES].T
        won[j * LANES:(j + 1) * LANES] = wo[:, j * LANES:(j + 1) * LANES].T
    forward(0)

    def halves_in(arr, img):
        for j in (2, 3):
            g_in(arr, img, j).wait_recv()

    def image_grads(img):
        halves_in(0, img)
        halves_in(1, img)
        proj = (dot(wq[...], gat[0, img]) + qbb[...]).astype(BF16)
        gmix = dot(wo[...], gat[1, img]).astype(BF16)
        for h in range(heads // HD):
            at = 3 * HD * h
            q = proj[at:at + HD]
            k = proj[at + HD:at + 2 * HD]
            val = proj[at + 2 * HD:at + 3 * HD]
            scores = dot_tn(k, q) * score_scale
            row = lax.broadcasted_iota(jnp.int32, scores.shape, 0)
            scores = jnp.where(row < tab[0, dp * slots + img], scores, -1e30)
            ex = jnp.exp(scores - jnp.max(scores, axis=0, keepdims=True))
            probs = ex / jnp.sum(ex, axis=0, keepdims=True)
            probs_b = probs.astype(BF16)
            mixs[h * HD:(h + 1) * HD] = dot(val, probs_b).astype(BF16)
            gm = gmix[h * HD:(h + 1) * HD]
            gprobs = dot_tn(val, gm)
            inner = jnp.sum(probs * gprobs, axis=0, keepdims=True)
            gscores = (probs * (gprobs - inner) * score_scale).astype(BF16)
            gpf[at:at + HD] = dot(k, gscores)
            gpf[at + HD:at + 2 * HD] = dot_nt(q, gscores)
            gpf[at + 2 * HD:at + 3 * HD] = dot_nt(gm, probs_b)
        gproj = gpf[...]
        qsum[...] += gproj
        osum[...] += gat[1, img, shard(grp)].astype(F32)
        gps[...] = gproj.astype(BF16)
        step = 2 * LANES
        for j in range(0, model, step):
            dq = dot_nt(gps[...], gat[0, img, j:j + step])
            do = dot_nt(mixs[...], gat[1, img, j:j + step])
            for i in range(0, step, LANES):
                at = (j + i) // LANES * both
                grad[at:at + qkv] += dq[:, i:i + LANES]
                grad[at + qkv:at + both] += do[:, i:i + LANES]

    def image_parts(img):
        op[img] = dot(won[...], mixs[...]).astype(BF16)
        ip[img] = dot(wqn[...], gps[...]).astype(BF16)

    def image(img, _):
        @pl.when(img + AHEAD < slots)
        def _():
            direct(img + AHEAD)

        @pl.when(img + 1 < slots)
        def _():
            forward(img + 1)

        image_grads(img)

        @pl.when(img + 1 < slots)
        def _():
            image_parts(img)

        return 0

    lax.fori_loop(0, slots, image, 0)
    qtot = jnp.sum(qsum[...].T, axis=0, keepdims=True)
    otot = jnp.sum(osum[...].T, axis=0, keepdims=True)
    for j in range(qtiles):
        w = min(LANES, qkv - j * LANES)
        grad[brow + j:brow + j + 1, :w] = qtot[:, j * LANES:j * LANES + w]
    for j in range(otiles):
        w = min(LANES, width - j * LANES)
        at = brow + qtiles + j
        grad[at:at + 1, :w] = otot[:, j * LANES:j * LANES + w]

    order = far_first(n) + [0]

    def piece(cc, s, p):
        return pl.ds(pl.multiple_of(((cc * STREAMS + s) * n + p) * piece_rows, TILE), piece_rows)

    def l0(s, k):
        p = plus(me[s % 2], k)
        return send(
            grad.at[piece(1 - c, s, p)], r0.at[s, p], b0s.at[s, k], b0r.at[s, k], other, grp
        )

    for k in order:
        for s in range(STREAMS):
            l0(s, k).start()
    image_parts(slots - 1)

    def x_copy(arr, img, j):
        src = (op, ip)[arr]
        ch = arr * slots + img
        ref, dst, to = (
            lambda: (src.at[img, lo_of(gx)], fw.at[ch, 0], gr),
            lambda: (src.at[img, hi_of(gx)], fw.at[ch, 1], gl),
            lambda: (src.at[img, hi_of(gr)], rcv.at[ch, 0, 1], gr),
            lambda: (src.at[img, lo_of(gl)], rcv.at[ch, 1, 0], gl),
            lambda: (mrg.at[ch, 0], rcv.at[ch, 0, 0], gr),
            lambda: (mrg.at[ch, 1], rcv.at[ch, 1, 1], gl),
        )[j]()
        return send(ref, dst, xs.at[ch, j], xr.at[ch, j], dp, to)

    def merge(arr):
        def step(img, _):
            ch = arr * slots + img
            src = (op, ip)[arr]
            x_copy(arr, img, 0).wait_recv()
            mrg[ch, 0] = (src[img, lo_of(gr)].astype(F32) + fw[ch, 0].astype(F32)).astype(BF16)
            x_copy(arr, img, 4).start()
            x_copy(arr, img, 1).wait_recv()
            mrg[ch, 1] = (src[img, hi_of(gl)].astype(F32) + fw[ch, 1].astype(F32)).astype(BF16)
            x_copy(arr, img, 5).start()
            return 0
        lax.fori_loop(0, slots, step, 0)

    for arr in (0, 1):
        def raw(img, _, arr=arr):
            for j in range(4):
                x_copy(arr, img, j).start()
            return 0
        lax.fori_loop(0, slots, raw, 0)

    def x_sent(first, last):
        for arr in (0, 1):
            def step(img, _, arr=arr):
                for j in range(first, last):
                    x_copy(arr, img, j).wait_send()
                return 0
            lax.fori_loop(0, slots, step, 0)

    def g_sent(img, _):
        for arr in (0, 1):
            for j in range(4):
                g_copy(arr, img, j).wait_send()
        return 0

    tree = n == 8
    cut = nb // 2 * TILE
    head_rows, tail_rows = pl.ds(0, cut), pl.ds(cut, piece_rows - cut)

    def l1(s, k):
        ref, dst, to = s1.at[s, k], r1.at[s, k], k
        if tree and k == 3:
            to = 1
        elif tree and k == 5:
            to = 7
        elif tree and k == 4:
            ref, dst, to = s1.at[s, 4, head_rows], r1.at[s, 4, head_rows], 2
        elif tree and k == 0:
            ref, dst, to = s1.at[s, 4, tail_rows], r1.at[s, 4, tail_rows], 6
        return send(ref, dst, b1s.at[s, k], b1r.at[s, k], on_axis(s % 2, plus(me[s % 2], to)), grp)

    for k in order:
        for s in range(STREAMS):
            l0(s, k).wait_recv()
            p = plus(me[s % 2], k)
            total = grad[piece(c, s, p)] + r0[s, p]
            if tree and k in (2, 6):
                m1[s, k // 4] = total
            elif k:
                s1[s, k] = total.astype(BF16)
                l1(s, k).start()
                if tree and k == 4:
                    l1(s, 0).start()
            else:
                t[s, pl.ds(0, piece_rows)] = total
                rest = part_rows * n - piece_rows
                if rest:
                    t[s, pl.ds(piece_rows, rest)] = jnp.zeros((rest, LANES), F32)

    if tree:
        for s in range(STREAMS):
            l1(s, 3).wait_recv()
            l1(s, 4).wait_recv()
            s1[s, 2, head_rows] = (
                m1[s, 0, head_rows] + r1[s, 3, head_rows].astype(F32) + r1[s, 4, head_rows].astype(F32)
            ).astype(BF16)
            s1[s, 2, tail_rows] = (m1[s, 0, tail_rows] + r1[s, 3, tail_rows].astype(F32)).astype(BF16)
            l1(s, 2).start()
            l1(s, 5).wait_recv()
            l1(s, 0).wait_recv()
            s1[s, 6, head_rows] = (m1[s, 1, head_rows] + r1[s, 5, head_rows].astype(F32)).astype(BF16)
            s1[s, 6, tail_rows] = (
                m1[s, 1, tail_rows] + r1[s, 5, tail_rows].astype(F32) + r1[s, 4, tail_rows].astype(F32)
            ).astype(BF16)
            l1(s, 6).start()

    lax.fori_loop(0, slots, g_sent, 0)
    for k in order:
        for s in range(STREAMS):
            l0(s, k).wait_send()

    def part(q):
        return pl.ds(pl.multiple_of(q * part_rows, TILE), part_rows)

    def l2(s, k):
        q = plus(me[1 - s % 2], k)
        return send(
            t.at[s, part(q)], r2.at[s, k], b2s.at[s, k], b2r.at[s, k], on_axis(1 - s % 2, q), grp,
        )

    near = list(reversed(far_first(n)))
    last = [1, 7, 2, 6] if tree else near
    for s in range(STREAMS):
        for k in last:
            l1(s, k).wait_recv()
        total = t[s, pl.ds(0, piece_rows)]
        for k in last:
            total = total + r1[s, k].astype(F32)
        t[s, pl.ds(0, piece_rows)] = total
        for k in far_first(n):
            l2(s, k).start()

    def l3(s, k):
        mine = v.at[s, part(me[1 - s % 2])]
        return send(
            mine, mine, b3s.at[s, k], b3r.at[s, k], on_axis(1 - s % 2, plus(me[1 - s % 2], k)), grp,
        )

    for s in range(STREAMS):
        for k in near:
            l2(s, k).wait_recv()
        total = t[s, part(me[1 - s % 2])]
        for k in near:
            total = total + r2[s, k]
        v[s, part(me[1 - s % 2])] = (total * scale).astype(BF16)
        for k in far_first(n):
            l3(s, k).start()

    merge(0)

    def some(cc, s, p, first, count):
        base = ((cc * STREAMS + s) * n + p) * piece_rows + first
        return pl.ds(pl.multiple_of(base, TILE), count)

    def l4(s, k):
        if not tree or k in (1, 2, 6, 7):
            ref, dst, to = v.at[s, pl.ds(0, piece_rows)], full.at[piece(c, s, me[s % 2])], k
        elif k in (3, 5):
            ref = dst = full.at[piece(c, s, plus(me[s % 2], 6 if k == 3 else 2))]
            to = 1 if k == 3 else 7
        elif k == 4:
            ref = dst = full.at[some(c, s, plus(me[s % 2], 6), 0, cut)]
            to = 2
        else:
            ref = dst = full.at[some(c, s, plus(me[s % 2], 2), cut, piece_rows - cut)]
            to = 6
        return send(ref, dst, b4s.at[s, k], b4r.at[s, k], on_axis(s % 2, plus(me[s % 2], to)), grp)

    def l5(s, k):
        at = full.at[piece(c, s, plus(me[s % 2], k))]
        return send(at, at, b5s.at[s, k], b5r.at[s, k], other, grp)

    def l3_in(s, k):
        at = v.at[s, part(plus(me[1 - s % 2], n - k))]
        return send(at, at, b3s.at[s, k], b3r.at[s, k], other, grp)

    for s in range(STREAMS):
        for k in near:
            l3_in(s, k).wait_recv()
        for k in ([2, 6, 1, 7] if tree else far_first(n)):
            l4(s, k).start()
        full[piece(c, s, me[s % 2])] = v[s, pl.ds(0, piece_rows)]
        l5(s, 0).start()

    merge(1)

    for k in range(n):
        for s in range(STREAMS):
            if k or tree:
                l1(s, k).wait_send()
            if k:
                l2(s, k).wait_send()
                l3(s, k).wait_send()
    x_sent(0, 4)

    def l4_in(s, k):
        at = full.at[piece(c, s, plus(me[s % 2], n - k))]
        if tree and k == 4:
            at = full.at[some(c, s, plus(me[s % 2], 4), 0, cut)]
        elif tree and k == 0:
            at = full.at[some(c, s, plus(me[s % 2], 4), cut, piece_rows - cut)]
        return send(at, at, b4s.at[s, k], b4r.at[s, k], other, grp)

    for k in ([2, 6, 1, 7, 3, 5, 4] if tree else near):
        for s in range(STREAMS):
            l4_in(s, k).wait_recv()
            if tree and k == 4:
                l4_in(s, 0).wait_recv()
            if tree and k in (2, 6):
                l4(s, 3 if k == 2 else 5).start()
                l4(s, 4 if k == 2 else 0).start()
            l5(s, n - k).start()

    def finish(arr):
        def step(img, _):
            ch = arr * slots + img
            for j in range(2, 6):
                x_copy(arr, img, j).wait_recv()
            src = (op, ip)[arr]
            total = src[img, shard(grp)].astype(F32)
            total = total + rcv[ch, 0].reshape(width, IMG).astype(F32)
            total = total + rcv[ch, 1].reshape(width, IMG).astype(F32)
            total = total + gat[arr, img, shard(grp)].astype(F32)
            if arr == 0:
                total = total + obb[...]
            total = jnp.where(lanes_below(img, total.shape), total, 0.0).astype(BF16)
            (lo_ref, ig_ref)[arr][:, pl.ds(pl.multiple_of(img * IMG, IMG), IMG)] = total
            return 0
        lax.fori_loop(0, slots, step, 0)

    finish(0)

    def l5_in(s, k):
        at = full.at[piece(1 - c, s, plus(me[s % 2], k))]
        return send(at, at, b5s.at[s, k], b5r.at[s, k], other, grp)

    for k in range(n):
        for s in range(STREAMS):
            l5_in(s, k).wait_recv()
    for j in range(tiles):
        at = j * both
        dq_ref[:, j * LANES:(j + 1) * LANES] = full[at:at + qkv]
        do_ref[:, j * LANES:(j + 1) * LANES] = full[at + qkv:at + both]
    sums = full[brow:brow + TILE].astype(F32)
    for ref, size, first in ((dqb_ref, qkv, 0), (dob_ref, width, qtiles)):
        for j in range(-(-size // LANES)):
            w = min(LANES, size - j * LANES)
            ref[j * LANES:j * LANES + w] = sums[first + j, :w]
    finish(1)
    for k in range(n):
        for s in range(STREAMS):
            l5(s, k).wait_send()
            if k or tree:
                l4(s, k).wait_send()
    x_sent(4, 6)


def store_all(count, *refs):
    copies = [
        pltpu.make_async_copy(refs[i], refs[count + i], refs[-1].at[i]) for i in range(count)
    ]
    for cp in copies:
        cp.start()
    for cp in copies:
        cp.wait()


def local(tokens, cotangent, slot_table, w_qkv, qkv_bias, w_out, out_bias):
    dp_count = lax.axis_size("dp")
    slots = slot_table.shape[0] // dp_count
    rows, width = tokens.shape
    model, qkv = w_qkv.shape
    heads = w_out.shape[0]
    n = math.isqrt(dp_count // 2)
    scale = 1.0 / math.sqrt(dp_count * slots * IMG)
    used = (qkv + heads) // TILE * (model // LANES) + 1
    nb = -(-used // (2 * STREAMS * n))
    nb2 = -(-nb // n)
    piece_rows, part_rows, half = nb * TILE, nb2 * TILE, width // 2
    chunks = 2 * slots
    vm = pl.BlockSpec(memory_space=pltpu.VMEM)
    hbm = pl.BlockSpec(memory_space=pltpu.HBM)
    dma = pltpu.SemaphoreType.DMA
    outs = pl.pallas_call(
        functools.partial(kernel, n, nb, nb2, slots, scale),
        out_shape=(
            jax.ShapeDtypeStruct((width, rows), BF16),
            jax.ShapeDtypeStruct((width, rows), BF16),
            jax.ShapeDtypeStruct((qkv, model), BF16),
            jax.ShapeDtypeStruct((qkv,), F32),
            jax.ShapeDtypeStruct((heads, model), BF16),
            jax.ShapeDtypeStruct((width,), F32),
        ),
        in_specs=[hbm] * 7,
        out_specs=(vm,) * 6,
        scratch_shapes=[
            pltpu.VMEM((2, slots, model, IMG), BF16),
            pltpu.VMEM((width, rows), BF16),
            pltpu.SMEM(slot_table.shape[::-1], jnp.int32),
            pltpu.VMEM((qkv, model), BF16),
            pltpu.VMEM((model, qkv), BF16),
            pltpu.VMEM((heads, model), BF16),
            pltpu.VMEM((model, heads), BF16),
            pltpu.VMEM((qkv,), F32),
            pltpu.VMEM((width,), F32),
            pltpu.VMEM((qkv, IMG), F32),
            pltpu.VMEM((width, IMG), F32),
            pltpu.VMEM((slots, model, IMG), BF16),
            pltpu.VMEM((slots, model, IMG), BF16),
            pltpu.VMEM((2 * STREAMS * n * piece_rows, LANES), F32),
            pltpu.VMEM((qkv, IMG), F32),
            pltpu.VMEM((qkv, IMG), F32),
            pltpu.VMEM((width, IMG), F32),
            pltpu.VMEM((qkv, IMG), BF16),
            pltpu.VMEM((heads, IMG), BF16),
            pltpu.VMEM((STREAMS, n, piece_rows, LANES), F32),
            pltpu.VMEM((STREAMS, n, piece_rows, LANES), BF16),
            pltpu.VMEM((STREAMS, n, piece_rows, LANES), BF16),
            pltpu.VMEM((STREAMS, 2, piece_rows, LANES), F32),
            pltpu.VMEM((STREAMS, n * part_rows, LANES), F32),
            pltpu.VMEM((STREAMS, n, part_rows, LANES), F32),
            pltpu.VMEM((STREAMS, n * part_rows, LANES), BF16),
            pltpu.VMEM((2 * STREAMS * n * piece_rows, LANES), BF16),
            pltpu.VMEM((chunks, 2, half, IMG), BF16),
            pltpu.VMEM((chunks, 2, half, IMG), BF16),
            pltpu.VMEM((chunks, 2, 2, half, IMG), BF16),
        ] + [dma((STREAMS, n))] * 12 + [dma((chunks, 6))] * 2 + [dma((chunks, 4))] * 2 + [dma((slots + 6,))],
        compiler_params=pltpu.CompilerParams(
            collective_id=0, has_side_effects=True, vmem_limit_bytes=50 * 2**20,
        ),
        cost_estimate=pl.CostEstimate(flops=4 * 10**9, bytes_accessed=10**7, transcendentals=0),
    )(*(
        pltpu.with_memory_space_constraint(a, pltpu.HBM)
        for a in (slot_table.T, tokens.T, cotangent.T, w_qkv.T, qkv_bias, w_out, out_bias)
    ))
    count = len(outs)
    outs = pl.pallas_call(
        functools.partial(store_all, count),
        out_shape=tuple(jax.ShapeDtypeStruct(o.shape, o.dtype) for o in outs),
        in_specs=[vm] * count,
        out_specs=(hbm,) * count,
        scratch_shapes=[dma((count,))],
        compiler_params=pltpu.CompilerParams(vmem_limit_bytes=8 * 2**20),
    )(*(pltpu.with_memory_space_constraint(o, pltpu.VMEM) for o in outs))
    layer_out, input_grad, dq, dqb, do, dob = outs
    return (layer_out.T, input_grad.T, dq.T, dqb, do, dob)


def solution(mesh):
    return jax.shard_map(
        local,
        mesh=mesh,
        in_specs=(
            P("dp", "group"),
            P("dp", "group"),
            P(),
            P(None, "group"),
            P("group"),
            P("group", None),
            P("group"),
        ),
        out_specs=(
            P("dp", "group"),
            P("dp", "group"),
            P(None, "group"),
            P("group"),
            P("group", None),
            P("group"),
        ),
        check_vma=False,
    )
```

```python
import functools
import math

import jax
import jax.numpy as jnp
from jax import lax
from jax.experimental import pallas as pl
from jax.experimental.pallas import tpu as pltpu
from jax.sharding import PartitionSpec as P

HD = 80
IMG = 128
GROUPS = 4
LANES = 128
TILE = 16
STREAMS = 2
AHEAD = 2
MESH = pl.DeviceIdType.MESH
BF16 = jnp.bfloat16
F32 = jnp.float32


def far_first(n):
    return sorted(range(1, n), key=lambda k: (-min(k, n - k), k))


def dot(a, b):
    return jnp.dot(a, b, preferred_element_type=F32)


def dot_nt(a, b):
    return lax.dot_general(a, b, (((1,), (1,)), ((), ())), preferred_element_type=F32)


def dot_tn(a, b):
    return lax.dot_general(a, b, (((0,), (0,)), ((), ())), preferred_element_type=F32)


def kernel(
    n, nb, nb2, slots, scale,
    tab_ref, x_ref, ct_ref, wq_ref, qb_ref, wo_ref, ob_ref,
    lo_ref, ig_ref, dq_ref, dqb_ref, do_ref, dob_ref,
    gat, ctv, tab, wq, wqn, wo, won, qb, ob, qbb, obb, op, ip, grad, gpf, qsum, osum, gps, mixs,
    r0, s1, r1, m1, t, r2, v, full, fw, mrg, rcv,
    b0s, b0r, b1s, b1r, b2s, b2r, b3s, b3r, b4s, b4r, b5s, b5r,
    xs, xr, gs, gr_sem, ls,
):
    width = x_ref.shape[0]
    model = width * GROUPS
    qkv = wq_ref.shape[0]
    heads = wo_ref.shape[0]
    both = qkv + heads
    tiles = model // LANES
    qtiles = -(-qkv // LANES)
    otiles = -(-width // LANES)
    brow = tiles * both
    piece_rows = nb * TILE
    part_rows = nb2 * TILE
    score_scale = 1.0 / math.sqrt(HD)

    dp = lax.axis_index("dp")
    grp = lax.axis_index("group")
    c = lax.rem(dp, 2)
    y = lax.rem(lax.div(dp, 2), n)
    z = lax.div(dp, 2 * n)
    other = dp + 1 - 2 * c
    gr = lax.rem(grp + 1, GROUPS)
    gl = lax.rem(grp + 3, GROUPS)
    gx = lax.rem(grp + 2, GROUPS)
    me = (y, z)

    def on_axis(axis, idx):
        return (z * n + idx) * 2 + c if axis == 0 else (idx * n + y) * 2 + c

    def plus(a, k):
        return lax.rem(a + k, n)

    def send(src, dst, ss, rs, d, g):
        return pltpu.make_async_remote_copy(
            src_ref=src, dst_ref=dst, send_sem=ss, recv_sem=rs,
            device_id=(d, g), device_id_type=MESH,
        )

    half = width // 2

    def shard(g):
        return pl.ds(pl.multiple_of(g * width, TILE), width)

    def lo_of(g):
        return pl.ds(pl.multiple_of(g * width, TILE), half)

    def hi_of(g):
        return pl.ds(pl.multiple_of(g * width + half, TILE), half)

    loads = [
        pltpu.make_async_copy(
            x_ref.at[:, i * IMG:(i + 1) * IMG], gat.at[0, i, shard(grp)], ls.at[i]
        )
        for i in range(slots)
    ]
    load_ct = pltpu.make_async_copy(ct_ref, ctv, ls.at[slots])
    load_wq = pltpu.make_async_copy(wq_ref, wq, ls.at[slots + 1])
    load_wo = pltpu.make_async_copy(wo_ref, wo, ls.at[slots + 2])
    load_tab = pltpu.make_async_copy(tab_ref, tab, ls.at[slots + 3])
    load_qb = pltpu.make_async_copy(qb_ref, qb, ls.at[slots + 4])
    load_ob = pltpu.make_async_copy(ob_ref, ob, ls.at[slots + 5])
    loads[0].start()
    load_tab.start()
    load_ct.start()

    barrier = pltpu.get_barrier_semaphore()
    for g in (gr, gl):
        pl.semaphore_signal(barrier, inc=1, device_id=(dp, g), device_id_type=MESH)
    pl.semaphore_signal(barrier, inc=1, device_id=(other, grp), device_id_type=MESH)
    for axis in (0, 1):
        for k in range(1, n):
            pl.semaphore_signal(
                barrier, inc=1, device_id=(on_axis(axis, plus(me[axis], k)), grp),
                device_id_type=MESH,
            )

    for cp in loads[1:]:
        cp.start()
    load_wq.start()
    load_wo.start()
    load_qb.start()
    load_ob.start()

    def lanes_below(img, shape):
        lane = lax.broadcasted_iota(jnp.int32, shape, 1)
        return lane < tab[0, dp * slots + img]

    def mask(i):
        rows = ctv[:, i * IMG:(i + 1) * IMG].astype(F32)
        gat[1, i, shard(grp)] = jnp.where(lanes_below(i, rows.shape), rows, 0.0).astype(BF16)

    def g_copy(arr, img, j):
        ch = arr * slots + img
        at, to = (
            lambda: (shard(grp), gr),
            lambda: (shard(grp), gl),
            lambda: (lo_of(gl), gr),
            lambda: (hi_of(gr), gl),
        )[j]()
        ref = gat.at[arr, img, at]
        return send(ref, ref, gs.at[ch, j], gr_sem.at[ch, j], dp, to)

    def g_in(arr, img, j):
        ch = arr * slots + img
        at = (lambda: shard(gl), lambda: shard(gr), lambda: lo_of(gx), lambda: hi_of(gx))[j]()
        ref = gat.at[arr, img, at]
        return send(ref, ref, gs.at[ch, j], gr_sem.at[ch, j], dp, gr)

    def direct(img, arrs=(0, 1)):
        for arr in arrs:
            for j in (0, 1):
                g_copy(arr, img, j).start()

    def forward(img):
        for arr in (0, 1):
            for j in (0, 1):
                g_in(arr, img, j).wait_recv()
                g_copy(arr, img, j + 2).start()

    pl.semaphore_wait(barrier, 1 + 2 * (n - 1) + 2)
    loads[0].wait()
    direct(0, (0,))
    load_tab.wait()
    load_ct.wait()
    mask(0)
    direct(0, (1,))
    for i in range(1, slots):
        loads[i].wait()
        mask(i)
        if i < AHEAD:
            direct(i)

    grad[...] = jnp.zeros(grad.shape, F32)
    qsum[...] = jnp.zeros(qsum.shape, F32)
    osum[...] = jnp.zeros(osum.shape, F32)
    load_qb.wait()
    load_ob.wait()
    load_wq.wait()
    load_wo.wait()
    qbb[...] = jnp.broadcast_to(qb[...].reshape(1, qkv), (IMG, qkv)).T
    obb[...] = jnp.broadcast_to(ob[...].reshape(1, width), (IMG, width)).T
    for j in range(tiles):
        wqn[j * LANES:(j + 1) * LANES] = wq[:, j * LANES:(j + 1) * LANES].T
        won[j * LANES:(j + 1) * LANES] = wo[:, j * LANES:(j + 1) * LANES].T
    forward(0)

    def halves_in(arr, img):
        for j in (2, 3):
            g_in(arr, img, j).wait_recv()

    def image_grads(img):
        halves_in(0, img)
        halves_in(1, img)
        proj = (dot(wq[...], gat[0, img]) + qbb[...]).astype(BF16)
        gmix = dot(wo[...], gat[1, img]).astype(BF16)
        for h in range(heads // HD):
            at = 3 * HD * h
            q = proj[at:at + HD]
            k = proj[at + HD:at + 2 * HD]
            val = proj[at + 2 * HD:at + 3 * HD]
            scores = dot_tn(k, q) * score_scale
            row = lax.broadcasted_iota(jnp.int32, scores.shape, 0)
            scores = jnp.where(row < tab[0, dp * slots + img], scores, -1e30)
            ex = jnp.exp(scores - jnp.max(scores, axis=0, keepdims=True))
            probs = ex / jnp.sum(ex, axis=0, keepdims=True)
            probs_b = probs.astype(BF16)
            mixs[h * HD:(h + 1) * HD] = dot(val, probs_b).astype(BF16)
            gm = gmix[h * HD:(h + 1) * HD]
            gprobs = dot_tn(val, gm)
            inner = jnp.sum(probs * gprobs, axis=0, keepdims=True)
            gscores = (probs * (gprobs - inner) * score_scale).astype(BF16)
            gpf[at:at + HD] = dot(k, gscores)
            gpf[at + HD:at + 2 * HD] = dot_nt(q, gscores)
            gpf[at + 2 * HD:at + 3 * HD] = dot_nt(gm, probs_b)
        gproj = gpf[...]
        qsum[...] += gproj
        osum[...] += gat[1, img, shard(grp)].astype(F32)
        gps[...] = gproj.astype(BF16)
        step = 2 * LANES
        for j in range(0, model, step):
            dq = dot_nt(gps[...], gat[0, img, j:j + step])
            do = dot_nt(mixs[...], gat[1, img, j:j + step])
            for i in range(0, step, LANES):
                at = (j + i) // LANES * both
                grad[at:at + qkv] += dq[:, i:i + LANES]
                grad[at + qkv:at + both] += do[:, i:i + LANES]

    def image_parts(img):
        op[img] = dot(won[...], mixs[...]).astype(BF16)
        ip[img] = dot(wqn[...], gps[...]).astype(BF16)

    def image(img, _):
        @pl.when(img + AHEAD < slots)
        def _():
            direct(img + AHEAD, (0,))

        @pl.when(img + 1 < slots)
        def _():
            forward(img + 1)

        @pl.when(img + AHEAD < slots)
        def _():
            direct(img + AHEAD, (1,))

        image_grads(img)

        @pl.when(img + 1 < slots)
        def _():
            image_parts(img)

        return 0

    lax.fori_loop(0, slots, image, 0)
    qtot = jnp.sum(qsum[...].T, axis=0, keepdims=True)
    otot = jnp.sum(osum[...].T, axis=0, keepdims=True)
    for j in range(qtiles):
        w = min(LANES, qkv - j * LANES)
        grad[brow + j:brow + j + 1, :w] = qtot[:, j * LANES:j * LANES + w]
    for j in range(otiles):
        w = min(LANES, width - j * LANES)
        at = brow + qtiles + j
        grad[at:at + 1, :w] = otot[:, j * LANES:j * LANES + w]

    order = far_first(n) + [0]

    def piece(cc, s, p):
        return pl.ds(pl.multiple_of(((cc * STREAMS + s) * n + p) * piece_rows, TILE), piece_rows)

    def l0(s, k):
        p = plus(me[s % 2], k)
        return send(
            grad.at[piece(1 - c, s, p)], r0.at[s, p], b0s.at[s, k], b0r.at[s, k], other, grp
        )

    for k in order:
        for s in range(STREAMS):
            l0(s, k).start()
    image_parts(slots - 1)

    def x_copy(arr, img, j):
        src = (op, ip)[arr]
        ch = arr * slots + img
        ref, dst, to = (
            lambda: (src.at[img, lo_of(gx)], fw.at[ch, 0], gr),
            lambda: (src.at[img, hi_of(gx)], fw.at[ch, 1], gl),
            lambda: (src.at[img, hi_of(gr)], rcv.at[ch, 0, 1], gr),
            lambda: (src.at[img, lo_of(gl)], rcv.at[ch, 1, 0], gl),
            lambda: (mrg.at[ch, 0], rcv.at[ch, 0, 0], gr),
            lambda: (mrg.at[ch, 1], rcv.at[ch, 1, 1], gl),
        )[j]()
        return send(ref, dst, xs.at[ch, j], xr.at[ch, j], dp, to)

    def merge(arr):
        def step(img, _):
            ch = arr * slots + img
            src = (op, ip)[arr]
            x_copy(arr, img, 0).wait_recv()
            mrg[ch, 0] = (src[img, lo_of(gr)].astype(F32) + fw[ch, 0].astype(F32)).astype(BF16)
            x_copy(arr, img, 4).start()
            x_copy(arr, img, 1).wait_recv()
            mrg[ch, 1] = (src[img, hi_of(gl)].astype(F32) + fw[ch, 1].astype(F32)).astype(BF16)
            x_copy(arr, img, 5).start()
            return 0
        lax.fori_loop(0, slots, step, 0)

    for arr in (0, 1):
        def raw(img, _, arr=arr):
            for j in range(4):
                x_copy(arr, img, j).start()
            return 0
        lax.fori_loop(0, slots, raw, 0)

    def x_sent(first, last):
        for arr in (0, 1):
            def step(img, _, arr=arr):
                for j in range(first, last):
                    x_copy(arr, img, j).wait_send()
                return 0
            lax.fori_loop(0, slots, step, 0)

    def g_sent(img, _):
        for arr in (0, 1):
            for j in range(4):
                g_copy(arr, img, j).wait_send()
        return 0

    tree = n == 8
    cut = nb // 2 * TILE
    head_rows, tail_rows = pl.ds(0, cut), pl.ds(cut, piece_rows - cut)

    def l1(s, k):
        ref, dst, to = s1.at[s, k], r1.at[s, k], k
        if tree and k == 3:
            to = 1
        elif tree and k == 5:
            to = 7
        elif tree and k == 4:
            ref, dst, to = s1.at[s, 4, head_rows], r1.at[s, 4, head_rows], 2
        elif tree and k == 0:
            ref, dst, to = s1.at[s, 4, tail_rows], r1.at[s, 4, tail_rows], 6
        return send(ref, dst, b1s.at[s, k], b1r.at[s, k], on_axis(s % 2, plus(me[s % 2], to)), grp)

    for k in order:
        for s in range(STREAMS):
            l0(s, k).wait_recv()
            p = plus(me[s % 2], k)
            total = grad[piece(c, s, p)] + r0[s, p]
            if tree and k in (2, 6):
                m1[s, k // 4] = total
            elif k:
                s1[s, k] = total.astype(BF16)
                l1(s, k).start()
                if tree and k == 4:
                    l1(s, 0).start()
            else:
                t[s, pl.ds(0, piece_rows)] = total
                rest = part_rows * n - piece_rows
                if rest:
                    t[s, pl.ds(piece_rows, rest)] = jnp.zeros((rest, LANES), F32)

    if tree:
        for s in range(STREAMS):
            l1(s, 3).wait_recv()
            l1(s, 4).wait_recv()
            s1[s, 2, head_rows] = (
                m1[s, 0, head_rows] + r1[s, 3, head_rows].astype(F32) + r1[s, 4, head_rows].astype(F32)
            ).astype(BF16)
            s1[s, 2, tail_rows] = (m1[s, 0, tail_rows] + r1[s, 3, tail_rows].astype(F32)).astype(BF16)
            l1(s, 2).start()
            l1(s, 5).wait_recv()
            l1(s, 0).wait_recv()
            s1[s, 6, head_rows] = (m1[s, 1, head_rows] + r1[s, 5, head_rows].astype(F32)).astype(BF16)
            s1[s, 6, tail_rows] = (
                m1[s, 1, tail_rows] + r1[s, 5, tail_rows].astype(F32) + r1[s, 4, tail_rows].astype(F32)
            ).astype(BF16)
            l1(s, 6).start()

    lax.fori_loop(0, slots, g_sent, 0)
    for k in order:
        for s in range(STREAMS):
            l0(s, k).wait_send()

    def part(q):
        return pl.ds(pl.multiple_of(q * part_rows, TILE), part_rows)

    def l2(s, k):
        q = plus(me[1 - s % 2], k)
        return send(
            t.at[s, part(q)], r2.at[s, k], b2s.at[s, k], b2r.at[s, k], on_axis(1 - s % 2, q), grp,
        )

    near = list(reversed(far_first(n)))
    last = [1, 7, 2, 6] if tree else near
    for s in range(STREAMS):
        for k in last:
            l1(s, k).wait_recv()
        total = t[s, pl.ds(0, piece_rows)]
        for k in last:
            total = total + r1[s, k].astype(F32)
        t[s, pl.ds(0, piece_rows)] = total
        for k in far_first(n):
            l2(s, k).start()

    def l3(s, k):
        mine = v.at[s, part(me[1 - s % 2])]
        return send(
            mine, mine, b3s.at[s, k], b3r.at[s, k], on_axis(1 - s % 2, plus(me[1 - s % 2], k)), grp,
        )

    for s in range(STREAMS):
        for k in near:
            l2(s, k).wait_recv()
        total = t[s, part(me[1 - s % 2])]
        for k in near:
            total = total + r2[s, k]
        v[s, part(me[1 - s % 2])] = (total * scale).astype(BF16)
        for k in far_first(n):
            l3(s, k).start()

    merge(0)

    def some(cc, s, p, first, count):
        base = ((cc * STREAMS + s) * n + p) * piece_rows + first
        return pl.ds(pl.multiple_of(base, TILE), count)

    def l4(s, k):
        if not tree or k in (1, 2, 6, 7):
            ref, dst, to = v.at[s, pl.ds(0, piece_rows)], full.at[piece(c, s, me[s % 2])], k
        elif k in (3, 5):
            ref = dst = full.at[piece(c, s, plus(me[s % 2], 6 if k == 3 else 2))]
            to = 1 if k == 3 else 7
        elif k == 4:
            ref = dst = full.at[some(c, s, plus(me[s % 2], 6), 0, cut)]
            to = 2
        else:
            ref = dst = full.at[some(c, s, plus(me[s % 2], 2), cut, piece_rows - cut)]
            to = 6
        return send(ref, dst, b4s.at[s, k], b4r.at[s, k], on_axis(s % 2, plus(me[s % 2], to)), grp)

    def l5(s, k):
        at = full.at[piece(c, s, plus(me[s % 2], k))]
        return send(at, at, b5s.at[s, k], b5r.at[s, k], other, grp)

    def l3_in(s, k):
        at = v.at[s, part(plus(me[1 - s % 2], n - k))]
        return send(at, at, b3s.at[s, k], b3r.at[s, k], other, grp)

    for s in range(STREAMS):
        for k in near:
            l3_in(s, k).wait_recv()
        for k in ([2, 6, 1, 7] if tree else far_first(n)):
            l4(s, k).start()
        full[piece(c, s, me[s % 2])] = v[s, pl.ds(0, piece_rows)]
        l5(s, 0).start()

    merge(1)

    for k in range(n):
        for s in range(STREAMS):
            if k or tree:
                l1(s, k).wait_send()
            if k:
                l2(s, k).wait_send()
                l3(s, k).wait_send()
    x_sent(0, 4)

    def l4_in(s, k):
        at = full.at[piece(c, s, plus(me[s % 2], n - k))]
        if tree and k == 4:
            at = full.at[some(c, s, plus(me[s % 2], 4), 0, cut)]
        elif tree and k == 0:
            at = full.at[some(c, s, plus(me[s % 2], 4), cut, piece_rows - cut)]
        return send(at, at, b4s.at[s, k], b4r.at[s, k], other, grp)

    for k in ([2, 6, 1, 7, 3, 5, 4] if tree else near):
        for s in range(STREAMS):
            l4_in(s, k).wait_recv()
            if tree and k == 4:
                l4_in(s, 0).wait_recv()
            if tree and k in (2, 6):
                l4(s, 3 if k == 2 else 5).start()
                l4(s, 4 if k == 2 else 0).start()
            l5(s, n - k).start()

    def finish(arr):
        def step(img, _):
            ch = arr * slots + img
            for j in range(2, 6):
                x_copy(arr, img, j).wait_recv()
            src = (op, ip)[arr]
            total = src[img, shard(grp)].astype(F32)
            total = total + rcv[ch, 0].reshape(width, IMG).astype(F32)
            total = total + rcv[ch, 1].reshape(width, IMG).astype(F32)
            total = total + gat[arr, img, shard(grp)].astype(F32)
            if arr == 0:
                total = total + obb[...]
            total = jnp.where(lanes_below(img, total.shape), total, 0.0).astype(BF16)
            (lo_ref, ig_ref)[arr][:, pl.ds(pl.multiple_of(img * IMG, IMG), IMG)] = total
            return 0
        lax.fori_loop(0, slots, step, 0)

    finish(0)

    def l5_in(s, k):
        at = full.at[piece(1 - c, s, plus(me[s % 2], k))]
        return send(at, at, b5s.at[s, k], b5r.at[s, k], other, grp)

    for k in range(n):
        for s in range(STREAMS):
            l5_in(s, k).wait_recv()
    for j in range(tiles):
        at = j * both
        dq_ref[:, j * LANES:(j + 1) * LANES] = full[at:at + qkv]
        do_ref[:, j * LANES:(j + 1) * LANES] = full[at + qkv:at + both]
    sums = full[brow:brow + TILE].astype(F32)
    for ref, size, first in ((dqb_ref, qkv, 0), (dob_ref, width, qtiles)):
        for j in range(-(-size // LANES)):
            w = min(LANES, size - j * LANES)
            ref[j * LANES:j * LANES + w] = sums[first + j, :w]
    finish(1)
    for k in range(n):
        for s in range(STREAMS):
            l5(s, k).wait_send()
            if k or tree:
                l4(s, k).wait_send()
    x_sent(4, 6)


def store_all(count, *refs):
    copies = [
        pltpu.make_async_copy(refs[i], refs[count + i], refs[-1].at[i]) for i in range(count)
    ]
    for cp in copies:
        cp.start()
    for cp in copies:
        cp.wait()


def local(tokens, cotangent, slot_table, w_qkv, qkv_bias, w_out, out_bias):
    dp_count = lax.axis_size("dp")
    slots = slot_table.shape[0] // dp_count
    rows, width = tokens.shape
    model, qkv = w_qkv.shape
    heads = w_out.shape[0]
    n = math.isqrt(dp_count // 2)
    scale = 1.0 / math.sqrt(dp_count * slots * IMG)
    used = (qkv + heads) // TILE * (model // LANES) + 1
    nb = -(-used // (2 * STREAMS * n))
    nb2 = -(-nb // n)
    piece_rows, part_rows, half = nb * TILE, nb2 * TILE, width // 2
    chunks = 2 * slots
    vm = pl.BlockSpec(memory_space=pltpu.VMEM)
    hbm = pl.BlockSpec(memory_space=pltpu.HBM)
    dma = pltpu.SemaphoreType.DMA
    outs = pl.pallas_call(
        functools.partial(kernel, n, nb, nb2, slots, scale),
        out_shape=(
            jax.ShapeDtypeStruct((width, rows), BF16),
            jax.ShapeDtypeStruct((width, rows), BF16),
            jax.ShapeDtypeStruct((qkv, model), BF16),
            jax.ShapeDtypeStruct((qkv,), F32),
            jax.ShapeDtypeStruct((heads, model), BF16),
            jax.ShapeDtypeStruct((width,), F32),
        ),
        in_specs=[hbm] * 7,
        out_specs=(vm,) * 6,
        scratch_shapes=[
            pltpu.VMEM((2, slots, model, IMG), BF16),
            pltpu.VMEM((width, rows), BF16),
            pltpu.SMEM(slot_table.shape[::-1], jnp.int32),
            pltpu.VMEM((qkv, model), BF16),
            pltpu.VMEM((model, qkv), BF16),
            pltpu.VMEM((heads, model), BF16),
            pltpu.VMEM((model, heads), BF16),
            pltpu.VMEM((qkv,), F32),
            pltpu.VMEM((width,), F32),
            pltpu.VMEM((qkv, IMG), F32),
            pltpu.VMEM((width, IMG), F32),
            pltpu.VMEM((slots, model, IMG), BF16),
            pltpu.VMEM((slots, model, IMG), BF16),
            pltpu.VMEM((2 * STREAMS * n * piece_rows, LANES), F32),
            pltpu.VMEM((qkv, IMG), F32),
            pltpu.VMEM((qkv, IMG), F32),
            pltpu.VMEM((width, IMG), F32),
            pltpu.VMEM((qkv, IMG), BF16),
            pltpu.VMEM((heads, IMG), BF16),
            pltpu.VMEM((STREAMS, n, piece_rows, LANES), F32),
            pltpu.VMEM((STREAMS, n, piece_rows, LANES), BF16),
            pltpu.VMEM((STREAMS, n, piece_rows, LANES), BF16),
            pltpu.VMEM((STREAMS, 2, piece_rows, LANES), F32),
            pltpu.VMEM((STREAMS, n * part_rows, LANES), F32),
            pltpu.VMEM((STREAMS, n, part_rows, LANES), F32),
            pltpu.VMEM((STREAMS, n * part_rows, LANES), BF16),
            pltpu.VMEM((2 * STREAMS * n * piece_rows, LANES), BF16),
            pltpu.VMEM((chunks, 2, half, IMG), BF16),
            pltpu.VMEM((chunks, 2, half, IMG), BF16),
            pltpu.VMEM((chunks, 2, 2, half, IMG), BF16),
        ] + [dma((STREAMS, n))] * 12 + [dma((chunks, 6))] * 2 + [dma((chunks, 4))] * 2 + [dma((slots + 6,))],
        compiler_params=pltpu.CompilerParams(
            collective_id=0, has_side_effects=True, vmem_limit_bytes=50 * 2**20,
        ),
        cost_estimate=pl.CostEstimate(flops=4 * 10**9, bytes_accessed=10**7, transcendentals=0),
    )(*(
        pltpu.with_memory_space_constraint(a, pltpu.HBM)
        for a in (slot_table.T, tokens.T, cotangent.T, w_qkv.T, qkv_bias, w_out, out_bias)
    ))
    count = len(outs)
    outs = pl.pallas_call(
        functools.partial(store_all, count),
        out_shape=tuple(jax.ShapeDtypeStruct(o.shape, o.dtype) for o in outs),
        in_specs=[vm] * count,
        out_specs=(hbm,) * count,
        scratch_shapes=[dma((count,))],
        compiler_params=pltpu.CompilerParams(vmem_limit_bytes=8 * 2**20),
    )(*(pltpu.with_memory_space_constraint(o, pltpu.VMEM) for o in outs))
    layer_out, input_grad, dq, dqb, do, dob = outs
    return (layer_out.T, input_grad.T, dq.T, dqb, do, dob)


def solution(mesh):
    return jax.shard_map(
        local,
        mesh=mesh,
        in_specs=(
            P("dp", "group"),
            P("dp", "group"),
            P(),
            P(None, "group"),
            P("group"),
            P("group", None),
            P("group"),
        ),
        out_specs=(
            P("dp", "group"),
            P("dp", "group"),
            P(None, "group"),
            P("group"),
            P("group", None),
            P("group"),
        ),
        check_vma=False,
    )
```
